32 devices in a mesh: tm: 8 (over z, x), space: 4 (over y, core).
Axes of the slice: x: 2, y: 2, z: 4, core: 2. Of those that a mesh axis runs over, the one named last changes fastest.
Arguments:
- iterate: float32 [8, 16, 512, 512], P('tm', None, 'space'), may hold values from -1.2 to 1.2
- start_state: float32 [512, 512], P('space'), may hold values from -1 to 1
- mobility: float32 [512], P('space'), may hold values from 0.5 to 2
- slot_element: int32 [4, 128], P('space'), may hold values from 0 to 127, each once within a row
Outputs:
- new_iterate: float32 [8, 16, 512, 512], P('tm', None, 'space')
The draws below stay inside these ranges and needn't reach their ends.
Inputs may be any that keep to these rules, and one draw needn't show every extreme that they name: Each row is a permutation of the 128 local elements of one device; slot k of device p stores the element of natural index slot_element[p, k].
All inputs are finite; a program needn't handle non-finite values.
Results may differ from the reference program's by a relative error of at most 0.00005.
Values sent between devices are 32-bit elements; how exact they have to be, the bound alone decides.
A program may use at most 128 MiB of HBM per device.

```python
import math
import jax
import jax.numpy as jnp
import numpy as np
from jax import lax

TN = 16
EX = 8
EY = 8
EZ_DEV = 2
NODES = 512
ELEM_DEV = 128
ELEMENTS = 512
SEGMENTS = 8
N_SPACE = 4


def block_levels(stream_key, extent, pieces, low, largest):
    loudness, own = 1.0, jax.random.fold_in(stream_key, 6)
    for position, parts in pieces:
        steps = jnp.exp(jax.random.uniform(jax.random.fold_in(own, position), (parts,), jnp.float32, low / len(pieces), largest / len(pieces)))
        loudness = loudness * jnp.repeat(steps, extent[position] // parts).reshape([-1 if axis == position else 1 for axis in range(len(extent))])
    return loudness


def setup_inputs(seed: int = 0) -> dict:
    keys = jax.random.split(jax.random.key(seed), 5)
    iterate = jnp.clip(jax.random.uniform(keys[0], (SEGMENTS, TN, ELEMENTS, NODES), jnp.float32, -1.2, 1.2) * block_levels(keys[0], (SEGMENTS, TN, ELEMENTS, NODES), ((0, 8), (2, 4)), -0.4, 0.0), -1.2, 1.2)
    start_state = jnp.clip(jax.random.uniform(keys[1], (ELEMENTS, NODES), jnp.float32, -1.0, 1.0) * block_levels(keys[1], (ELEMENTS, NODES), ((0, 4),), -0.4, 0.0), -1.0, 1.0)
    mobility = jnp.clip(jnp.exp(math.log(2.0) - 1.3862944 * jax.random.uniform(keys[2], (ELEMENTS,), jnp.float32) ** block_levels(keys[2], (ELEMENTS,), ((0, 4),), -0.2, 0.2)), 0.5, 2.0)
    slot_element = jax.vmap(lambda own: jax.random.permutation(own, ELEM_DEV))(jax.random.split(keys[3], N_SPACE)).reshape((N_SPACE, ELEM_DEV)).astype(jnp.int32)
    return dict(iterate=iterate, start_state=start_state, mobility=mobility, slot_element=slot_element)


REACTION_RATE = 4.0
DIFFUSIVITY = 0.002
SEGMENT_SPAN = 0.1


def legendre_rows(points, order_n):
    table = np.zeros((points.shape[0], order_n + 1))
    table[:, 0] = 1.0
    table[:, 1] = points
    for k in range(2, order_n + 1):
        table[:, k] = ((2 * k - 1) * points * table[:, k - 1] - (k - 1) * table[:, k - 2]) / k
    return table


def spectral_tables(time_count):
    order_n = 7
    points = -np.cos(np.pi * np.arange(order_n + 1) / order_n)
    for _ in range(60):
        legendre = legendre_rows(points, order_n)
        points = points - (points * legendre[:, order_n] - legendre[:, order_n - 1]) / ((order_n + 1) * legendre[:, order_n])
    legendre = legendre_rows(points, order_n)
    top_poly = legendre[:, order_n]
    weights = 2.0 / (order_n * (order_n + 1) * top_poly ** 2)
    derivative = np.zeros((order_n + 1, order_n + 1))
    for i in range(order_n + 1):
        for j in range(order_n + 1):
            if i != j:
                derivative[i, j] = top_poly[i] / (top_poly[j] * (points[i] - points[j]))
    derivative[0, 0] = -order_n * (order_n + 1) / 4.0
    derivative[order_n, order_n] = order_n * (order_n + 1) / 4.0
    stiff_1d = derivative.T @ (weights[:, None] * derivative)
    mass_1d = np.zeros((order_n + 1, order_n + 1))
    mass_1d[np.arange(order_n + 1), np.arange(order_n + 1)] = weights
    stiffness = 0.5 * (np.kron(np.kron(stiff_1d, mass_1d), mass_1d) + np.kron(np.kron(mass_1d, stiff_1d), mass_1d) + np.kron(np.kron(mass_1d, mass_1d), stiff_1d))
    mass_diag = 0.125 * np.kron(np.kron(weights, weights), weights)
    angles = np.pi - np.pi * np.arange(time_count) / (time_count - 1)
    cheb_nodes = np.cos(angles)
    vandermonde = np.cos(np.outer(angles, np.arange(time_count)))
    degree = time_count - 1
    half_ends = np.ones(time_count)
    half_ends[0] = 0.5
    half_ends[degree] = 0.5
    inverse_v = (2.0 / degree) * vandermonde.T * half_ends[None, :] * half_ends[:, None]
    integral_table = np.zeros((time_count, time_count))
    integral_table[:, 0] = cheb_nodes + 1.0
    integral_table[:, 1] = 0.5 * (cheb_nodes ** 2 - 1.0)
    for n in range(2, time_count):
        upper_term = np.cos((n + 1) * angles) / (n + 1) - np.cos((n - 1) * angles) / (n - 1)
        lower_term = (-1.0) ** (n + 1) / (n + 1) - (-1.0) ** (n - 1) / (n - 1)
        integral_table[:, n] = 0.5 * (upper_term - lower_term)
    quadrature = 0.5 * SEGMENT_SPAN * integral_table @ inverse_v
    return (jnp.asarray(stiffness, jnp.float32), jnp.asarray(mass_diag, jnp.float32), jnp.asarray(quadrature, jnp.float32))


def shift_elements(array, elem_axis, direction):
    length = array.shape[elem_axis]
    zero_slab = jnp.zeros_like(lax.slice_in_dim(array, 0, 1, axis=elem_axis))
    if direction > 0:
        return jnp.concatenate([lax.slice_in_dim(array, 1, length, axis=elem_axis), zero_slab], axis=elem_axis)
    return jnp.concatenate([zero_slab, lax.slice_in_dim(array, 0, length - 1, axis=elem_axis)], axis=elem_axis)


def assemble(array, elem_axis, stride):
    node_level = (jnp.arange(array.shape[-1]) // stride) % 8
    from_next = jnp.roll(shift_elements(array, elem_axis, 1), 7 * stride, axis=-1)
    from_prev = jnp.roll(shift_elements(array, elem_axis, -1), -7 * stride, axis=-1)
    return array + jnp.where(node_level == 7, from_next, 0.0) + jnp.where(node_level == 0, from_prev, 0.0)


def assemble_all(array):
    return assemble(assemble(assemble(array, -2, 1), -3, 8), -4, 64)


def reference(iterate, start_state, mobility, slot_element):
    stiffness, mass_diag, quadrature = spectral_tables(TN)
    total_layers = EZ_DEV * N_SPACE
    slot_order = (slot_element + (jnp.arange(N_SPACE, dtype=jnp.int32) * ELEM_DEV)[:, None]).reshape(-1).astype(jnp.int32)
    natural_order = jnp.argsort(slot_order).astype(jnp.int32)
    mass_nat = assemble_all(jnp.broadcast_to(mass_diag, (1, total_layers, EY, EX, NODES)))
    mass_store = mass_nat.reshape(ELEMENTS, NODES)[slot_order]

    def segment_terms(values):
        scaled = values * mobility[None, :, None]
        natural = scaled[:, natural_order]
        stiff_flux = jnp.dot(natural.reshape(-1, NODES), stiffness, precision=lax.Precision.HIGHEST)
        stiff_flux = assemble_all(stiff_flux.reshape(TN, total_layers, EY, EX, NODES))
        flux_store = stiff_flux.reshape(TN, ELEMENTS, NODES)[:, slot_order]
        time_rate = REACTION_RATE * (values - values * values * values) - DIFFUSIVITY * flux_store / mass_store
        integral = jnp.dot(quadrature, time_rate.reshape(TN, -1), precision=lax.Precision.HIGHEST)
        return integral.reshape(TN, ELEMENTS, NODES)

    integrals = lax.map(segment_terms, iterate)
    increments = integrals[:, -1]
    running = jnp.cumsum(increments, axis=0)
    earlier = jnp.concatenate([jnp.zeros_like(increments[:1]), running[:-1]], axis=0)
    return (start_state[None, None] + earlier[:, None]) + integrals
```

```python
import functools

import jax
import jax.numpy as jnp
import ml_dtypes
import numpy as np
from jax import lax
from jax.experimental import pallas as pl
from jax.experimental.pallas import tpu as pltpu
from jax.sharding import PartitionSpec as P

EX = 8
EY = 8
EZ_DEV = 2
NODES = 512


REACTION_RATE = 4.0
DIFFUSIVITY = 0.002
SEGMENT_SPAN = 0.1
T_BLOCK = 4
ROLL = pltpu.roll


def legendre_rows(points, order_n):
    table = np.zeros((points.shape[0], order_n + 1))
    table[:, 0] = 1.0
    table[:, 1] = points
    for k in range(2, order_n + 1):
        table[:, k] = ((2 * k - 1) * points * table[:, k - 1] - (k - 1) * table[:, k - 2]) / k
    return table


def spectral_tables(time_count):
    order_n = 7
    points = -np.cos(np.pi * np.arange(order_n + 1) / order_n)
    for _ in range(60):
        legendre = legendre_rows(points, order_n)
        points = points - (points * legendre[:, order_n] - legendre[:, order_n - 1]) / (
            (order_n + 1) * legendre[:, order_n]
        )
    legendre = legendre_rows(points, order_n)
    top_poly = legendre[:, order_n]
    weights = 2.0 / (order_n * (order_n + 1) * top_poly**2)
    derivative = np.zeros((order_n + 1, order_n + 1))
    for i in range(order_n + 1):
        for j in range(order_n + 1):
            if i != j:
                derivative[i, j] = top_poly[i] / (top_poly[j] * (points[i] - points[j]))
    derivative[0, 0] = -order_n * (order_n + 1) / 4.0
    derivative[order_n, order_n] = order_n * (order_n + 1) / 4.0
    stiff_1d = derivative.T @ (weights[:, None] * derivative)
    mass_1d = np.zeros((order_n + 1, order_n + 1))
    mass_1d[np.arange(order_n + 1), np.arange(order_n + 1)] = weights
    stiffness = 0.5 * (
        np.kron(np.kron(stiff_1d, mass_1d), mass_1d)
        + np.kron(np.kron(mass_1d, stiff_1d), mass_1d)
        + np.kron(np.kron(mass_1d, mass_1d), stiff_1d)
    )
    angles = np.pi - np.pi * np.arange(time_count) / (time_count - 1)
    cheb_nodes = np.cos(angles)
    vandermonde = np.cos(np.outer(angles, np.arange(time_count)))
    degree = time_count - 1
    half_ends = np.ones(time_count)
    half_ends[0] = 0.5
    half_ends[degree] = 0.5
    inverse_v = 2.0 / degree * vandermonde.T * half_ends[None, :] * half_ends[:, None]
    integral_table = np.zeros((time_count, time_count))
    integral_table[:, 0] = cheb_nodes + 1.0
    integral_table[:, 1] = 0.5 * (cheb_nodes**2 - 1.0)
    for n in range(2, time_count):
        upper_term = np.cos((n + 1) * angles) / (n + 1) - np.cos((n - 1) * angles) / (n - 1)
        lower_term = (-1.0) ** (n + 1) / (n + 1) - (-1.0) ** (n - 1) / (n - 1)
        integral_table[:, n] = 0.5 * (upper_term - lower_term)
    quadrature = 0.5 * SEGMENT_SPAN * integral_table @ inverse_v
    return stiffness, weights, quadrature


def split(table):
    high = table.astype(ml_dtypes.bfloat16)
    return high, (table - high.astype(np.float64)).astype(ml_dtypes.bfloat16)


def halves(value):
    high = value.astype(jnp.bfloat16)
    return high, (value - high.astype(jnp.float32)).astype(jnp.bfloat16)


def mm(a, b):
    return jnp.dot(a, b, preferred_element_type=jnp.float32)


def mm3(a, b):
    return mm(a[0], b[0]) + (mm(a[1], b[0]) + mm(a[0], b[1]))


def flux_factor(weights):
    def assembled(count, ends):
        table = np.tile(weights, (count, 1))
        shared = weights[0] + weights[-1]
        table[1:, 0] = shared
        table[:-1, -1] = shared
        if not ends:
            table[0, 0] = shared
            table[-1, -1] = shared
        return table

    z, y, x = assembled(EZ_DEV, False), assembled(EY, True), assembled(EX, True)
    mass = 0.125 * np.einsum("ai,bj,ck->abcijk", z, y, x)
    return (-DIFFUSIVITY / mass).reshape(EZ_DEV * EY * EX, NODES).astype(np.float32)


def flux_kernel(
    end_ratio, slot_row, slot_col, mobility, values, k_high, k_low, factor, rate, up, down
):
    count, elems = values.shape[0], values.shape[1]
    layer = elems // 2
    position = lax.axis_index("space")
    low_end = jnp.where(position == 0, end_ratio, 1.0).astype(jnp.float32)
    high_end = jnp.where(position == lax.axis_size("space") - 1, end_ratio, 1.0).astype(jnp.float32)
    square = (elems, elems)
    to_natural = (slot_row[...] == lax.broadcasted_iota(jnp.int32, square, 0)).astype(jnp.float32).astype(jnp.bfloat16)
    to_store = (slot_col[...] == lax.broadcasted_iota(jnp.int32, square, 1)).astype(jnp.float32).astype(jnp.bfloat16)
    rows = []
    for t in range(count):
        scaled = halves(values[t] * mobility[...])
        rows.append([mm(to_natural, part).astype(jnp.bfloat16) for part in scaled])
    natural = [jnp.concatenate([row[i] for row in rows], axis=0) for i in range(2)]
    flux = mm3(natural, (k_high[...], k_low[...]))

    cube = (elems // 8, 8, 128)
    lane = lax.broadcasted_iota(jnp.int32, cube, 2)
    ex = lax.broadcasted_iota(jnp.int32, cube, 1)
    ey = lax.broadcasted_iota(jnp.int32, cube, 0) % 8
    kx, ky = lane % 8, lane // 8 % 8
    x_next, x_prev = (kx == 7) & (ex < 7), (kx == 0) & (ex > 0)
    y_next, y_prev = (ky == 7) & (ey < 7), (ky == 0) & (ey > 0)
    left = lax.broadcasted_iota(jnp.int32, (layer, 128), 1) < 64
    left_half = lax.broadcasted_iota(jnp.int32, (layer // 2, 128), 1) < 64
    for t in range(count):
        columns = []
        for c in range(4):
            f = flux[t * elems : (t + 1) * elems, c * 128 : (c + 1) * 128].reshape(cube)
            f = (
                f
                + jnp.where(x_next, ROLL(ROLL(f, 7, 2), 7, 1), 0.0)
                + jnp.where(x_prev, ROLL(ROLL(f, 121, 2), 1, 1), 0.0)
            )
            after, before = ROLL(f, 56, 2), ROLL(f, 72, 2)
            after = jnp.concatenate([after[1:], after[:1]], axis=0)
            before = jnp.concatenate([before[-1:], before[:-1]], axis=0)
            f = f + jnp.where(y_next, after, 0.0) + jnp.where(y_prev, before, 0.0)
            columns.append(f.reshape(elems, 128) * factor[:, c * 128 : (c + 1) * 128])
        first, last = columns[0], columns[3]
        bottom, top = first[:layer], last[layer:]
        half = layer // 2
        up[t] = jnp.where(left_half, ROLL(top[:half], 64, 1), top[half:])
        down[t] = jnp.where(left_half, bottom[half:], ROLL(bottom[:half], 64, 1))
        first_top = first[layer:] + jnp.where(left, ROLL(last[:layer], 64, 1), 0.0)
        last_bottom = last[:layer] + jnp.where(left, 0.0, ROLL(first[layer:], 64, 1))
        columns[0] = jnp.concatenate([jnp.where(left, bottom * low_end, bottom), first_top], axis=0)
        columns[3] = jnp.concatenate([last_bottom, jnp.where(left, top, top * high_end)], axis=0)
        high, low = halves(jnp.concatenate(columns, axis=1))
        stored = mm(to_store, high) + mm(to_store, low)
        v = values[t]
        rate[t] = REACTION_RATE * (v - v * v * v) + stored


def time_kernel(q_high, q_low, rate, integral):
    count, elems, nodes = rate.shape
    for block in range(elems // 8):
        part = rate[:, block * 8 : block * 8 + 8, :].reshape(count * 8, nodes)
        done = mm3((q_high[...], q_low[...]), halves(part))
        integral[:, block * 8 : block * 8 + 8, :] = done.reshape(count, 8, nodes)


def store_face(slot_col, face):
    layer = face.shape[0]
    elem = lax.broadcasted_iota(jnp.int32, (2 * layer, layer), 1)
    high, low = halves(face)
    columns = []
    for first in (0, layer):
        pick = (slot_col[...] == elem + first).astype(jnp.float32).astype(jnp.bfloat16)
        columns.append(mm(pick, high) + mm(pick, low))
    left = lax.broadcasted_iota(jnp.int32, columns[0].shape, 1) < 64
    return jnp.where(left, columns[0], 0.0), jnp.where(left, 0.0, columns[1])


def face_kernel(slot_col, q_high, q_low, below, above, inner, faces, increment):
    count, half, lanes = below.shape
    left = lax.broadcasted_iota(jnp.int32, (count, half, lanes), 2) < 64
    lower, upper = below[...], above[...]
    face = jnp.concatenate(
        [
            jnp.where(left, lower, upper),
            jnp.where(left, ROLL(lower, 64, 2), ROLL(upper, 64, 2)),
        ],
        axis=1,
    )
    for block in range(2 * half // 8):
        part = face[:, block * 8 : block * 8 + 8, :].reshape(count * 8, lanes)
        done = mm3((q_high[...], q_low[...]), halves(part))
        faces[:, block * 8 : block * 8 + 8, :] = done.reshape(count, 8, lanes)
    first, last = store_face(slot_col, faces[count - 1])
    increment[...] = inner[0]
    increment[:, :128] += first
    increment[:, 384:] += last


def final_kernel(slot_col, base, faces, integral, out):
    for t in range(integral.shape[0]):
        first, last = store_face(slot_col, faces[t])
        whole = base[...] + integral[t]
        out[t, :, :128] = whole[:, :128] + first
        out[t, :, 128:384] = whole[:, 128:384]
        out[t, :, 384:] = whole[:, 384:] + last


def neighbours(block, step):
    count = lax.axis_size("space")
    pairs = [(i, i + step) for i in range(count) if 0 <= i + step < count]
    return lax.ppermute(block, "space", pairs)


def earlier_sum(part):
    gathered = lax.all_gather(part, "tm")
    index = jnp.arange(gathered.shape[0])[:, None, None]
    return jnp.sum(jnp.where(index < lax.axis_index("tm"), gathered, 0.0), axis=0)


def whole_block(*shape):
    return pl.BlockSpec(shape, lambda i: (0,) * len(shape))


def cost(flops, moved):
    return pl.CostEstimate(flops=flops, bytes_accessed=moved, transcendentals=0)


def on_device(iterate, start_state, mobility, slot_element):
    values = iterate[0]
    count, elems, nodes = values.shape
    stiffness, weights, quadrature = spectral_tables(count)
    k_high, k_low = split(stiffness)
    q_high, q_low = split(np.kron(quadrature, np.eye(8)))
    factor = flux_factor(weights)
    end_ratio = float((weights[0] + weights[-1]) / weights[0])
    slot_row = slot_element.reshape(1, elems)
    slot_col = slot_element.reshape(elems, 1)
    half = elems // 4
    f32 = jnp.float32
    params = pltpu.CompilerParams(vmem_limit_bytes=40 * 2**20)
    field = jax.ShapeDtypeStruct((count, elems, nodes), f32)
    face_shape = jax.ShapeDtypeStruct((count, half, 128), f32)
    times = pl.BlockSpec((T_BLOCK, elems, nodes), lambda i: (i, 0, 0))
    face_times = pl.BlockSpec((T_BLOCK, half, 128), lambda i: (i, 0, 0))
    size = count * elems * nodes
    rate, up, down = pl.pallas_call(
        functools.partial(flux_kernel, end_ratio),
        out_shape=(field, face_shape, face_shape),
        grid=(count // T_BLOCK,),
        in_specs=[
            whole_block(1, elems),
            whole_block(elems, 1),
            whole_block(elems, 1),
            times,
            whole_block(nodes, nodes),
            whole_block(nodes, nodes),
            whole_block(elems, nodes),
        ],
        out_specs=(times, face_times, face_times),
        compiler_params=params,
        cost_estimate=cost(6 * size * nodes, 8 * size),
        name="flux",
    )(slot_row, slot_col, mobility.reshape(elems, 1), values, k_high, k_low, factor)
    below = neighbours(up, 1)
    above = neighbours(down, -1)
    q_spec = whole_block(8 * count, 8 * count)
    rows = pl.BlockSpec((count, 32, nodes), lambda i: (0, i, 0))
    integral = pl.pallas_call(
        time_kernel,
        out_shape=field,
        grid=(elems // 32,),
        in_specs=[q_spec, q_spec, rows],
        out_specs=rows,
        compiler_params=params,
        cost_estimate=cost(6 * size * 128, 8 * size),
        name="quadrature",
    )(q_high, q_low, rate)
    faces, increment = pl.pallas_call(
        face_kernel,
        out_shape=(
            jax.ShapeDtypeStruct((count, 2 * half, 128), f32),
            jax.ShapeDtypeStruct((elems, nodes), f32),
        ),
        grid=(1,),
        in_specs=[
            whole_block(elems, 1),
            q_spec,
            q_spec,
            whole_block(count, half, 128),
            whole_block(count, half, 128),
            pl.BlockSpec((1, elems, nodes), lambda i: (count - 1, 0, 0)),
        ],
        out_specs=(whole_block(count, 2 * half, 128), whole_block(elems, nodes)),
        compiler_params=params,
        name="faces",
    )(slot_col, q_high, q_low, below, above, integral)
    base = start_state + earlier_sum(increment)
    result = pl.pallas_call(
        final_kernel,
        out_shape=field,
        grid=(count // T_BLOCK,),
        in_specs=[
            whole_block(elems, 1),
            whole_block(elems, nodes),
            pl.BlockSpec((T_BLOCK, 2 * half, 128), lambda i: (i, 0, 0)),
            times,
        ],
        out_specs=times,
        compiler_params=params,
        name="final",
    )(slot_col, base, faces, integral)
    return result[None]


def solution(mesh):
    in_specs = (P("tm", None, "space", None), P("space", None), P("space"), P("space", None))
    out_specs = P("tm", None, "space", None)
    return jax.shard_map(
        on_device, mesh=mesh, in_specs=in_specs, out_specs=out_specs, check_vma=False
    )
```

```python
import functools

import jax
import jax.numpy as jnp
import ml_dtypes
import numpy as np
from jax import lax
from jax.experimental import pallas as pl
from jax.experimental.pallas import tpu as pltpu
from jax.sharding import PartitionSpec as P

EX = 8
EY = 8
EZ_DEV = 2
NODES = 512


REACTION_RATE = 4.0
DIFFUSIVITY = 0.002
SEGMENT_SPAN = 0.1
T_BLOCK = 4
ROLL = pltpu.roll


def legendre_rows(points, order_n):
    table = np.zeros((points.shape[0], order_n + 1))
    table[:, 0] = 1.0
    table[:, 1] = points
    for k in range(2, order_n + 1):
        table[:, k] = ((2 * k - 1) * points * table[:, k - 1] - (k - 1) * table[:, k - 2]) / k
    return table


def spectral_tables(time_count):
    order_n = 7
    points = -np.cos(np.pi * np.arange(order_n + 1) / order_n)
    for _ in range(60):
        legendre = legendre_rows(points, order_n)
        points = points - (points * legendre[:, order_n] - legendre[:, order_n - 1]) / (
            (order_n + 1) * legendre[:, order_n]
        )
    legendre = legendre_rows(points, order_n)
    top_poly = legendre[:, order_n]
    weights = 2.0 / (order_n * (order_n + 1) * top_poly**2)
    derivative = np.zeros((order_n + 1, order_n + 1))
    for i in range(order_n + 1):
        for j in range(order_n + 1):
            if i != j:
                derivative[i, j] = top_poly[i] / (top_poly[j] * (points[i] - points[j]))
    derivative[0, 0] = -order_n * (order_n + 1) / 4.0
    derivative[order_n, order_n] = order_n * (order_n + 1) / 4.0
    stiff_1d = derivative.T @ (weights[:, None] * derivative)
    mass_1d = np.zeros((order_n + 1, order_n + 1))
    mass_1d[np.arange(order_n + 1), np.arange(order_n + 1)] = weights
    stiffness = 0.5 * (
        np.kron(np.kron(stiff_1d, mass_1d), mass_1d)
        + np.kron(np.kron(mass_1d, stiff_1d), mass_1d)
        + np.kron(np.kron(mass_1d, mass_1d), stiff_1d)
    )
    angles = np.pi - np.pi * np.arange(time_count) / (time_count - 1)
    cheb_nodes = np.cos(angles)
    vandermonde = np.cos(np.outer(angles, np.arange(time_count)))
    degree = time_count - 1
    half_ends = np.ones(time_count)
    half_ends[0] = 0.5
    half_ends[degree] = 0.5
    inverse_v = 2.0 / degree * vandermonde.T * half_ends[None, :] * half_ends[:, None]
    integral_table = np.zeros((time_count, time_count))
    integral_table[:, 0] = cheb_nodes + 1.0
    integral_table[:, 1] = 0.5 * (cheb_nodes**2 - 1.0)
    for n in range(2, time_count):
        upper_term = np.cos((n + 1) * angles) / (n + 1) - np.cos((n - 1) * angles) / (n - 1)
        lower_term = (-1.0) ** (n + 1) / (n + 1) - (-1.0) ** (n - 1) / (n - 1)
        integral_table[:, n] = 0.5 * (upper_term - lower_term)
    quadrature = 0.5 * SEGMENT_SPAN * integral_table @ inverse_v
    return stiffness, weights, quadrature


def split(table):
    high = table.astype(ml_dtypes.bfloat16)
    return high, (table - high.astype(np.float64)).astype(ml_dtypes.bfloat16)


def halves(value):
    high = value.astype(jnp.bfloat16)
    return high, (value - high.astype(jnp.float32)).astype(jnp.bfloat16)


def mm(a, b):
    return jnp.dot(a, b, preferred_element_type=jnp.float32)


def mm3(a, b):
    return mm(a[0], b[0]) + (mm(a[1], b[0]) + mm(a[0], b[1]))


def flux_factor(weights):
    def assembled(count, ends):
        table = np.tile(weights, (count, 1))
        shared = weights[0] + weights[-1]
        table[1:, 0] = shared
        table[:-1, -1] = shared
        if not ends:
            table[0, 0] = shared
            table[-1, -1] = shared
        return table

    z, y, x = assembled(EZ_DEV, False), assembled(EY, True), assembled(EX, True)
    mass = 0.125 * np.einsum("ai,bj,ck->abcijk", z, y, x)
    return (-DIFFUSIVITY / mass).reshape(EZ_DEV * EY * EX, NODES).astype(np.float32)


def column(row, mask):
    return jnp.sum(jnp.where(mask, row.astype(jnp.float32), 0.0), axis=1, keepdims=True)


def slots_as_column(slot_row):
    square = (slot_row.shape[1], slot_row.shape[1])
    same = lax.broadcasted_iota(jnp.int32, square, 0) == lax.broadcasted_iota(jnp.int32, square, 1)
    return column(slot_row[...], same).astype(jnp.int32)


def one_hot(mask):
    return mask.astype(jnp.float32).astype(jnp.bfloat16)


def flux_kernel(
    end_ratio, slot_row, mobility, values, k_high, k_low, factor, rate, up, down
):
    count, elems = values.shape[0], values.shape[1]
    layer = elems // 2
    position = lax.axis_index("space")
    low_end = jnp.where(position == 0, end_ratio, 1.0).astype(jnp.float32)
    high_end = jnp.where(position == lax.axis_size("space") - 1, end_ratio, 1.0).astype(jnp.float32)
    square = (elems, elems)
    place = slot_row[...] == lax.broadcasted_iota(jnp.int32, square, 0)
    natural_mobility = column(mobility[...], place)
    to_natural = one_hot(place)
    to_store = one_hot(slots_as_column(slot_row) == lax.broadcasted_iota(jnp.int32, square, 1))
    rows = []
    for t in range(count):
        scaled = halves(values[t])
        rows.append([mm(to_natural, part).astype(jnp.bfloat16) for part in scaled])
    natural = [jnp.concatenate([row[i] for row in rows], axis=0) for i in range(2)]
    flux = mm3(natural, (k_high[...], k_low[...]))

    cube = (elems // 8, 8, 128)
    lane = lax.broadcasted_iota(jnp.int32, cube, 2)
    ex = lax.broadcasted_iota(jnp.int32, cube, 1)
    ey = lax.broadcasted_iota(jnp.int32, cube, 0) % 8
    kx, ky = lane % 8, lane // 8 % 8
    x_next, x_prev = (kx == 7) & (ex < 7), (kx == 0) & (ex > 0)
    y_next, y_prev = (ky == 7) & (ey < 7), (ky == 0) & (ey > 0)
    left = lax.broadcasted_iota(jnp.int32, (layer, 128), 1) < 64
    left_half = lax.broadcasted_iota(jnp.int32, (layer // 2, 128), 1) < 64
    for t in range(count):
        columns = []
        for c in range(4):
            f = flux[t * elems : (t + 1) * elems, c * 128 : (c + 1) * 128]
            f = (f * natural_mobility).reshape(cube)
            f = (
                f
                + jnp.where(x_next, ROLL(ROLL(f, 7, 2), 7, 1), 0.0)
                + jnp.where(x_prev, ROLL(ROLL(f, 121, 2), 1, 1), 0.0)
            )
            after, before = ROLL(f, 56, 2), ROLL(f, 72, 2)
            after = jnp.concatenate([after[1:], after[:1]], axis=0)
            before = jnp.concatenate([before[-1:], before[:-1]], axis=0)
            f = f + jnp.where(y_next, after, 0.0) + jnp.where(y_prev, before, 0.0)
            columns.append(f.reshape(elems, 128) * factor[:, c * 128 : (c + 1) * 128])
        first, last = columns[0], columns[3]
        bottom, top = first[:layer], last[layer:]
        half = layer // 2
        up[t] = jnp.where(left_half, ROLL(top[:half], 64, 1), top[half:])
        down[t] = jnp.where(left_half, bottom[half:], ROLL(bottom[:half], 64, 1))
        first_top = first[layer:] + jnp.where(left, ROLL(last[:layer], 64, 1), 0.0)
        last_bottom = last[:layer] + jnp.where(left, 0.0, ROLL(first[layer:], 64, 1))
        columns[0] = jnp.concatenate([jnp.where(left, bottom * low_end, bottom), first_top], axis=0)
        columns[3] = jnp.concatenate([last_bottom, jnp.where(left, top, top * high_end)], axis=0)
        high, low = halves(jnp.concatenate(columns, axis=1))
        stored = mm(to_store, high) + mm(to_store, low)
        v = values[t]
        rate[t] = REACTION_RATE * (v - v * v * v) + stored


def time_kernel(q_high, q_low, rate, integral):
    count, elems, nodes = rate.shape
    for block in range(elems // 8):
        part = rate[:, block * 8 : block * 8 + 8, :].reshape(count * 8, nodes)
        done = mm3((q_high[...], q_low[...]), halves(part))
        integral[:, block * 8 : block * 8 + 8, :] = done.reshape(count, 8, nodes)


def store_face(slots, face):
    layer = face.shape[0]
    elem = lax.broadcasted_iota(jnp.int32, (2 * layer, layer), 1)
    high, low = halves(face)
    columns = []
    for first in (0, layer):
        pick = one_hot(slots == elem + first)
        columns.append(mm(pick, high) + mm(pick, low))
    left = lax.broadcasted_iota(jnp.int32, columns[0].shape, 1) < 64
    return jnp.where(left, columns[0], 0.0), jnp.where(left, 0.0, columns[1])


def face_kernel(slot_row, q_high, q_low, below, above, inner, faces, increment):
    count, half, lanes = below.shape
    left = lax.broadcasted_iota(jnp.int32, (count, half, lanes), 2) < 64
    lower, upper = below[...], above[...]
    face = jnp.concatenate(
        [
            jnp.where(left, lower, upper),
            jnp.where(left, ROLL(lower, 64, 2), ROLL(upper, 64, 2)),
        ],
        axis=1,
    )
    for block in range(2 * half // 8):
        part = face[:, block * 8 : block * 8 + 8, :].reshape(count * 8, lanes)
        done = mm3((q_high[...], q_low[...]), halves(part))
        faces[:, block * 8 : block * 8 + 8, :] = done.reshape(count, 8, lanes)
    first, last = store_face(slots_as_column(slot_row), faces[count - 1])
    increment[...] = inner[0]
    increment[:, :128] += first
    increment[:, 384:] += last


def final_kernel(slot_row, base, faces, integral, out):
    slots = slots_as_column(slot_row)
    for t in range(integral.shape[0]):
        first, last = store_face(slots, faces[t])
        whole = base[...] + integral[t]
        out[t, :, :128] = whole[:, :128] + first
        out[t, :, 128:384] = whole[:, 128:384]
        out[t, :, 384:] = whole[:, 384:] + last


def neighbours(block, step):
    count = lax.axis_size("space")
    pairs = [(i, i + step) for i in range(count) if 0 <= i + step < count]
    return lax.ppermute(block, "space", pairs)


def prefix_kernel(rows, cols, increment, start, base, arrived, sums, earlier, sent, got, returned, back):
    n = lax.axis_size("tm")
    me = lax.axis_index("tm")
    splits = increment.shape[1] // cols

    def piece(ref, j):
        if splits == 1:
            return ref.at[pl.ds(pl.multiple_of(j * rows, 8), rows), :]
        return ref.at[
            pl.ds(pl.multiple_of(j // splits * rows, 8), rows),
            pl.ds(pl.multiple_of(j % splits * cols, 128), cols),
        ]

    def outward(j, source):
        return pltpu.make_async_remote_copy(
            src_ref=piece(increment, j),
            dst_ref=arrived.at[source],
            send_sem=sent.at[j],
            recv_sem=got.at[source],
            device_id={"tm": j},
            device_id_type=pl.DeviceIdType.MESH,
        )

    def homeward(j, owner):
        return pltpu.make_async_remote_copy(
            src_ref=sums.at[j],
            dst_ref=piece(earlier, owner),
            send_sem=returned.at[j],
            recv_sem=back.at[owner],
            device_id={"tm": j},
            device_id_type=pl.DeviceIdType.MESH,
        )

    def others(action):
        def one(d, carry):
            action(lax.rem(me + d, n))
            return carry

        lax.fori_loop(1, n, one, 0)

    barrier = pltpu.get_barrier_semaphore()
    others(
        lambda j: pl.semaphore_signal(
            barrier, inc=1, device_id={"tm": j}, device_id_type=pl.DeviceIdType.MESH
        )
    )
    pl.semaphore_wait(barrier, n - 1)

    @pl.when(me < n - 1)
    def _():
        others(lambda j: outward(j, me).start())

    def hand_out(i, running):
        @pl.when(i != me)
        def _():
            sums[i] = running
            homeward(i, me).start()

        @pl.when(i == me)
        def _():
            piece(earlier, me)[...] = running

    def add(i, running):
        @pl.when(i != me)
        def _():
            outward(i, i).wait_recv()

        @pl.when(i == me)
        def _():
            arrived[i] = piece(increment, me)[...]

        running = running + arrived[i]
        hand_out(i + 1, running)
        return running

    lax.fori_loop(0, n - 1, add, jnp.zeros((rows, cols), jnp.float32))

    @pl.when(me == 0)
    def _():
        base[...] = start[...]

    @pl.when(me > 0)
    def _():
        others(lambda j: homeward(j, j).wait_recv())
        base[...] = start[...] + earlier[...]

    @pl.when(me < n - 1)
    def _():
        others(lambda j: outward(j, me).wait_send())

    def sent_home(j):
        @pl.when(j > 0)
        def _():
            homeward(j, me).wait_send()

    others(sent_home)


def start_and_earlier(increment, start_state):
    elems, nodes = increment.shape
    n = lax.axis_size("tm")
    rows = max(8, elems // n)
    cols = nodes * elems // (rows * n)
    piece = (n, rows, cols)
    return pl.pallas_call(
        functools.partial(prefix_kernel, rows, cols),
        out_shape=jax.ShapeDtypeStruct(increment.shape, jnp.float32),
        in_specs=[pl.BlockSpec(memory_space=pltpu.VMEM)] * 2,
        out_specs=pl.BlockSpec(memory_space=pltpu.VMEM),
        scratch_shapes=[
            pltpu.VMEM(piece, jnp.float32),
            pltpu.VMEM(piece, jnp.float32),
            pltpu.VMEM(increment.shape, jnp.float32),
        ]
        + [pltpu.SemaphoreType.DMA((n,))] * 4,
        compiler_params=pltpu.CompilerParams(collective_id=0, has_side_effects=True),
        name="prefix",
    )(increment, start_state)


def whole_block(*shape):
    return pl.BlockSpec(shape, lambda i: (0,) * len(shape))


def cost(flops, moved):
    return pl.CostEstimate(flops=flops, bytes_accessed=moved, transcendentals=0)


def on_device(iterate, start_state, mobility, slot_element):
    values = iterate[0]
    count, elems, nodes = values.shape
    stiffness, weights, quadrature = spectral_tables(count)
    k_high, k_low = split(stiffness)
    q_high, q_low = split(np.kron(quadrature, np.eye(8)))
    factor = flux_factor(weights)
    end_ratio = float((weights[0] + weights[-1]) / weights[0])
    slot_row = slot_element.reshape(1, elems)
    half = elems // 4
    f32 = jnp.float32
    params = pltpu.CompilerParams(vmem_limit_bytes=24 * 2**20)
    field = jax.ShapeDtypeStruct((count, elems, nodes), f32)
    face_shape = jax.ShapeDtypeStruct((count, half, 128), f32)
    times = pl.BlockSpec((T_BLOCK, elems, nodes), lambda i: (i, 0, 0))
    face_times = pl.BlockSpec((T_BLOCK, half, 128), lambda i: (i, 0, 0))
    size = count * elems * nodes
    rate, up, down = pl.pallas_call(
        functools.partial(flux_kernel, end_ratio),
        out_shape=(field, face_shape, face_shape),
        grid=(count // T_BLOCK,),
        in_specs=[
            whole_block(1, elems),
            whole_block(1, elems),
            times,
            whole_block(nodes, nodes),
            whole_block(nodes, nodes),
            whole_block(elems, nodes),
        ],
        out_specs=(times, face_times, face_times),
        compiler_params=pltpu.CompilerParams(vmem_limit_bytes=60 * 2**20),
        cost_estimate=cost(6 * size * nodes, 8 * size),
        name="flux",
    )(slot_row, mobility.reshape(1, elems), values, k_high, k_low, factor)
    below = neighbours(up, 1)
    above = neighbours(down, -1)
    q_spec = whole_block(8 * count, 8 * count)
    rows = pl.BlockSpec((count, 32, nodes), lambda i: (0, i, 0))
    integral = pl.pallas_call(
        time_kernel,
        out_shape=field,
        grid=(elems // 32,),
        in_specs=[q_spec, q_spec, rows],
        out_specs=rows,
        compiler_params=params,
        cost_estimate=cost(6 * size * 128, 8 * size),
        name="quadrature",
    )(q_high, q_low, rate)
    faces, increment = pl.pallas_call(
        face_kernel,
        out_shape=(
            jax.ShapeDtypeStruct((count, 2 * half, 128), f32),
            jax.ShapeDtypeStruct((elems, nodes), f32),
        ),
        grid=(1,),
        in_specs=[
            whole_block(1, elems),
            q_spec,
            q_spec,
            whole_block(count, half, 128),
            whole_block(count, half, 128),
            pl.BlockSpec((1, elems, nodes), lambda i: (count - 1, 0, 0)),
        ],
        out_specs=(whole_block(count, 2 * half, 128), whole_block(elems, nodes)),
        compiler_params=params,
        name="faces",
    )(slot_row, q_high, q_low, below, above, integral)
    base = start_and_earlier(increment, start_state)
    result = pl.pallas_call(
        final_kernel,
        out_shape=field,
        grid=(count // T_BLOCK,),
        in_specs=[
            whole_block(1, elems),
            whole_block(elems, nodes),
            pl.BlockSpec((T_BLOCK, 2 * half, 128), lambda i: (i, 0, 0)),
            times,
        ],
        out_specs=times,
        compiler_params=params,
        name="final",
    )(slot_row, base, faces, integral)
    return result[None]


def solution(mesh):
    in_specs = (P("tm", None, "space", None), P("space", None), P("space"), P("space", None))
    out_specs = P("tm", None, "space", None)
    return jax.shard_map(
        on_device, mesh=mesh, in_specs=in_specs, out_specs=out_specs, check_vma=False
    )
```

```python
import functools

import jax
import jax.numpy as jnp
import ml_dtypes
import numpy as np
from jax import lax
from jax.experimental import pallas as pl
from jax.experimental.pallas import tpu as pltpu
from jax.sharding import PartitionSpec as P

EX = 8
EY = 8
EZ_DEV = 2
NODES = 512


REACTION_RATE = 4.0
DIFFUSIVITY = 0.002
SEGMENT_SPAN = 0.1
T_BLOCK = 4
ROLL = pltpu.roll


def legendre_rows(points, order_n):
    table = np.zeros((points.shape[0], order_n + 1))
    table[:, 0] = 1.0
    table[:, 1] = points
    for k in range(2, order_n + 1):
        table[:, k] = ((2 * k - 1) * points * table[:, k - 1] - (k - 1) * table[:, k - 2]) / k
    return table


def spectral_tables(time_count):
    order_n = 7
    points = -np.cos(np.pi * np.arange(order_n + 1) / order_n)
    for _ in range(60):
        legendre = legendre_rows(points, order_n)
        points = points - (points * legendre[:, order_n] - legendre[:, order_n - 1]) / (
            (order_n + 1) * legendre[:, order_n]
        )
    legendre = legendre_rows(points, order_n)
    top_poly = legendre[:, order_n]
    weights = 2.0 / (order_n * (order_n + 1) * top_poly**2)
    derivative = np.zeros((order_n + 1, order_n + 1))
    for i in range(order_n + 1):
        for j in range(order_n + 1):
            if i != j:
                derivative[i, j] = top_poly[i] / (top_poly[j] * (points[i] - points[j]))
    derivative[0, 0] = -order_n * (order_n + 1) / 4.0
    derivative[order_n, order_n] = order_n * (order_n + 1) / 4.0
    stiff_1d = derivative.T @ (weights[:, None] * derivative)
    mass_1d = np.zeros((order_n + 1, order_n + 1))
    mass_1d[np.arange(order_n + 1), np.arange(order_n + 1)] = weights
    stiffness = 0.5 * (
        np.kron(np.kron(stiff_1d, mass_1d), mass_1d)
        + np.kron(np.kron(mass_1d, stiff_1d), mass_1d)
        + np.kron(np.kron(mass_1d, mass_1d), stiff_1d)
    )
    angles = np.pi - np.pi * np.arange(time_count) / (time_count - 1)
    cheb_nodes = np.cos(angles)
    vandermonde = np.cos(np.outer(angles, np.arange(time_count)))
    degree = time_count - 1
    half_ends = np.ones(time_count)
    half_ends[0] = 0.5
    half_ends[degree] = 0.5
    inverse_v = 2.0 / degree * vandermonde.T * half_ends[None, :] * half_ends[:, None]
    integral_table = np.zeros((time_count, time_count))
    integral_table[:, 0] = cheb_nodes + 1.0
    integral_table[:, 1] = 0.5 * (cheb_nodes**2 - 1.0)
    for n in range(2, time_count):
        upper_term = np.cos((n + 1) * angles) / (n + 1) - np.cos((n - 1) * angles) / (n - 1)
        lower_term = (-1.0) ** (n + 1) / (n + 1) - (-1.0) ** (n - 1) / (n - 1)
        integral_table[:, n] = 0.5 * (upper_term - lower_term)
    quadrature = 0.5 * SEGMENT_SPAN * integral_table @ inverse_v
    return stiffness, weights, quadrature


def split(table):
    high = table.astype(ml_dtypes.bfloat16)
    return high, (table - high.astype(np.float64)).astype(ml_dtypes.bfloat16)


def halves(value):
    high = value.astype(jnp.bfloat16)
    return high, (value - high.astype(jnp.float32)).astype(jnp.bfloat16)


def mm(a, b):
    return jnp.dot(a, b, preferred_element_type=jnp.float32)


def mm3(a, b):
    return mm(a[0], b[0]) + (mm(a[1], b[0]) + mm(a[0], b[1]))


def flux_factor(weights):
    def assembled(count, ends):
        table = np.tile(weights, (count, 1))
        shared = weights[0] + weights[-1]
        table[1:, 0] = shared
        table[:-1, -1] = shared
        if not ends:
            table[0, 0] = shared
            table[-1, -1] = shared
        return table

    z, y, x = assembled(EZ_DEV, False), assembled(EY, True), assembled(EX, True)
    mass = 0.125 * np.einsum("ai,bj,ck->abcijk", z, y, x)
    return (-DIFFUSIVITY / mass).reshape(EZ_DEV * EY * EX, NODES).astype(np.float32)


def column(row, mask):
    return jnp.sum(jnp.where(mask, row.astype(jnp.float32), 0.0), axis=1, keepdims=True)


def slots_as_column(slot_row):
    square = (slot_row.shape[1], slot_row.shape[1])
    same = lax.broadcasted_iota(jnp.int32, square, 0) == lax.broadcasted_iota(jnp.int32, square, 1)
    return column(slot_row[...], same).astype(jnp.int32)


def one_hot(mask):
    return mask.astype(jnp.float32).astype(jnp.bfloat16)


def flux_kernel(
    end_ratio, slot_row, mobility, values, k_high, k_low, factor, rate, up, down
):
    count, elems = values.shape[0], values.shape[1]
    layer = elems // 2
    position = lax.axis_index("space")
    low_end = jnp.where(position == 0, end_ratio, 1.0).astype(jnp.float32)
    high_end = jnp.where(position == lax.axis_size("space") - 1, end_ratio, 1.0).astype(jnp.float32)
    square = (elems, elems)
    place = slot_row[...] == lax.broadcasted_iota(jnp.int32, square, 0)
    natural_mobility = column(mobility[...], place)
    to_natural = one_hot(place)
    to_store = one_hot(slots_as_column(slot_row) == lax.broadcasted_iota(jnp.int32, square, 1))
    rows = []
    for t in range(count):
        scaled = halves(values[t])
        rows.append([mm(to_natural, part).astype(jnp.bfloat16) for part in scaled])
    natural = [jnp.concatenate([row[i] for row in rows], axis=0) for i in range(2)]
    flux = mm3(natural, (k_high[...], k_low[...]))

    cube = (elems // 8, 8, 128)
    lane = lax.broadcasted_iota(jnp.int32, cube, 2)
    ex = lax.broadcasted_iota(jnp.int32, cube, 1)
    ey = lax.broadcasted_iota(jnp.int32, cube, 0) % 8
    kx, ky = lane % 8, lane // 8 % 8
    x_next, x_prev = (kx == 7) & (ex < 7), (kx == 0) & (ex > 0)
    y_next, y_prev = (ky == 7) & (ey < 7), (ky == 0) & (ey > 0)
    left = lax.broadcasted_iota(jnp.int32, (layer, 128), 1) < 64
    left_half = lax.broadcasted_iota(jnp.int32, (layer // 2, 128), 1) < 64
    for t in range(count):
        columns = []
        for c in range(4):
            f = flux[t * elems : (t + 1) * elems, c * 128 : (c + 1) * 128]
            f = (f * natural_mobility).reshape(cube)
            f = (
                f
                + jnp.where(x_next, ROLL(ROLL(f, 7, 2), 7, 1), 0.0)
                + jnp.where(x_prev, ROLL(ROLL(f, 121, 2), 1, 1), 0.0)
            )
            after, before = ROLL(f, 56, 2), ROLL(f, 72, 2)
            after = jnp.concatenate([after[1:], after[:1]], axis=0)
            before = jnp.concatenate([before[-1:], before[:-1]], axis=0)
            f = f + jnp.where(y_next, after, 0.0) + jnp.where(y_prev, before, 0.0)
            columns.append(f.reshape(elems, 128) * factor[:, c * 128 : (c + 1) * 128])
        first, last = columns[0], columns[3]
        bottom, top = first[:layer], last[layer:]
        half = layer // 2
        up[t] = jnp.where(left_half, ROLL(top[:half], 64, 1), top[half:])
        down[t] = jnp.where(left_half, bottom[half:], ROLL(bottom[:half], 64, 1))
        first_top = first[layer:] + jnp.where(left, ROLL(last[:layer], 64, 1), 0.0)
        last_bottom = last[:layer] + jnp.where(left, 0.0, ROLL(first[layer:], 64, 1))
        columns[0] = jnp.concatenate([jnp.where(left, bottom * low_end, bottom), first_top], axis=0)
        columns[3] = jnp.concatenate([last_bottom, jnp.where(left, top, top * high_end)], axis=0)
        high, low = halves(jnp.concatenate(columns, axis=1))
        stored = mm(to_store, high) + mm(to_store, low)
        v = values[t]
        rate[t] = REACTION_RATE * (v - v * v * v) + stored


def store_face(slots, face):
    layer = face.shape[0]
    elem = lax.broadcasted_iota(jnp.int32, (2 * layer, layer), 1)
    high, low = halves(face)
    columns = []
    for first in (0, layer):
        pick = one_hot(slots == elem + first)
        columns.append(mm(pick, high) + mm(pick, low))
    left = lax.broadcasted_iota(jnp.int32, columns[0].shape, 1) < 64
    return jnp.where(left, columns[0], 0.0), jnp.where(left, 0.0, columns[1])


def final_kernel(slot_row, base, faces, integral, out):
    slots = slots_as_column(slot_row)
    for t in range(integral.shape[0]):
        first, last = store_face(slots, faces[t])
        whole = base[...] + integral[t]
        out[t, :, :128] = whole[:, :128] + first
        out[t, :, 128:384] = whole[:, 128:384]
        out[t, :, 384:] = whole[:, 384:] + last


def exchange_kernel(
    last_row, slot_row, q_high, q_low, start, up, down, rate, base, faces, integral,
    held, below, above, increment, arrived, sums, earlier,
    loaded, face_sent, face_got, sent, got, returned, back,
):
    n, me = lax.axis_size("tm"), lax.axis_index("tm")
    extent, position = lax.axis_size("space"), lax.axis_index("space")
    count, elems, nodes = held.shape
    rows = arrived.shape[2]
    owners = elems // rows
    mesh_id = pl.DeviceIdType.MESH

    def piece(ref, part, j):
        return ref.at[part, pl.ds(pl.multiple_of(j * rows, 8), rows), :]

    def outward(part, j, source):
        return pltpu.make_async_remote_copy(
            src_ref=piece(increment, part, j),
            dst_ref=arrived.at[part, source],
            send_sem=sent.at[part, j],
            recv_sem=got.at[part, source],
            device_id={"tm": j},
            device_id_type=mesh_id,
        )

    def homeward(part, j, owner):
        return pltpu.make_async_remote_copy(
            src_ref=sums.at[part, j],
            dst_ref=piece(earlier, part, owner),
            send_sem=returned.at[part, j],
            recv_sem=back.at[part, owner],
            device_id={"tm": j},
            device_id_type=mesh_id,
        )

    def face_copy(source, target, which, step):
        return pltpu.make_async_remote_copy(
            src_ref=source,
            dst_ref=target,
            send_sem=face_sent.at[which],
            recv_sem=face_got.at[which],
            device_id={"space": position + step},
            device_id_type=mesh_id,
        )

    def others(action):
        def one(d, carry):
            action(lax.rem(me + d, n))
            return carry

        lax.fori_loop(1, n, one, 0)

    def when(condition, action):
        pl.when(condition)(action)

    def other_owners(action):
        if owners == n:
            others(action)
        else:
            others(lambda j: when(j < owners, lambda: action(j)))

    def send_increment(part):
        @pl.when(me < n - 1)
        def _():
            other_owners(lambda j: outward(part, j, me).start())

    def scan(part):
        def hand_out(i, running):
            @pl.when(i != me)
            def _():
                sums[part, i] = running
                homeward(part, i, me).start()

            @pl.when(i == me)
            def _():
                piece(earlier, part, me)[...] = running

        def add(i, running):
            @pl.when(i != me)
            def _():
                outward(part, i, i).wait_recv()

            @pl.when(i == me)
            def _():
                arrived[part, i] = piece(increment, part, me)[...]

            running = running + arrived[part, i]
            hand_out(i + 1, running)
            return running

        def own():
            lax.fori_loop(0, n - 1, add, jnp.zeros(arrived.shape[2:], jnp.float32))

        if owners == n:
            own()
        else:
            when(me < owners, own)

    load = pltpu.make_async_copy(rate, held, loaded)
    load.start()
    barrier = pltpu.get_barrier_semaphore()

    def greet(device):
        pl.semaphore_signal(barrier, inc=1, device_id=device, device_id_type=mesh_id)

    others(lambda j: greet({"tm": j}))
    has_below, has_above = position > 0, position < extent - 1
    when(has_below, lambda: greet({"space": position - 1}))
    when(has_above, lambda: greet({"space": position + 1}))
    pl.semaphore_wait(barrier, n - 1 + has_below.astype(jnp.int32) + has_above.astype(jnp.int32))

    when(has_above, lambda: face_copy(up, below, 0, 1).start())
    when(has_below, lambda: face_copy(down, above, 1, -1).start())
    load.wait()
    total = last_row[0] * held[0, :, 128:384]
    for t in range(1, count):
        total = total + last_row[t] * held[t, :, 128:384]
    increment[0] = total
    send_increment(0)

    width = 32

    def quadrature(index, carry):
        for k in range(width // 8):
            these = pl.ds(pl.multiple_of(index * width + k * 8, 8), 8)
            part = held[:, these, :].reshape(count * 8, nodes)
            done = mm3((q_high[...], q_low[...]), halves(part))
            integral[:, these, :] = done.reshape(count, 8, nodes)
        return carry

    lax.fori_loop(0, elems // width, quadrature, 0)

    @pl.when(has_below)
    def _():
        face_copy(up, below, 0, 1).wait_recv()

    @pl.when(position == 0)
    def _():
        below[...] = jnp.zeros_like(below)

    @pl.when(has_above)
    def _():
        face_copy(down, above, 1, -1).wait_recv()

    @pl.when(position == extent - 1)
    def _():
        above[...] = jnp.zeros_like(above)

    left = lax.broadcasted_iota(jnp.int32, below.shape, 2) < 64
    lower, upper = below[...], above[...]
    face = jnp.concatenate(
        [
            jnp.where(left, lower, upper),
            jnp.where(left, ROLL(lower, 64, 2), ROLL(upper, 64, 2)),
        ],
        axis=1,
    )
    for block in range(face.shape[1] // 8):
        part = face[:, block * 8 : block * 8 + 8, :].reshape(count * 8, 128)
        done = mm3((q_high[...], q_low[...]), halves(part))
        faces[:, block * 8 : block * 8 + 8, :] = done.reshape(count, 8, 128)
    first, last = store_face(slots_as_column(slot_row), faces[count - 1])
    increment[1, :, :128] = integral[count - 1, :, :128] + first
    increment[1, :, 128:] = integral[count - 1, :, 384:] + last
    send_increment(1)
    scan(0)
    scan(1)

    @pl.when(me == 0)
    def _():
        base[...] = start[...]

    @pl.when(me > 0)
    def _():
        for part in range(2):
            other_owners(lambda j: homeward(part, j, j).wait_recv())
        base[:, :128] = start[:, :128] + earlier[1, :, :128]
        base[:, 128:384] = start[:, 128:384] + earlier[0]
        base[:, 384:] = start[:, 384:] + earlier[1, :, 128:]

    when(has_above, lambda: face_copy(up, below, 0, 1).wait_send())
    when(has_below, lambda: face_copy(down, above, 1, -1).wait_send())

    def sent_home(part, j):
        when(j > 0, lambda: homeward(part, j, me).wait_send())

    for part in range(2):

        @pl.when(me < n - 1)
        def _():
            other_owners(lambda j: outward(part, j, me).wait_send())

        def all_home():
            others(lambda j: sent_home(part, j))

        if owners == n:
            all_home()
        else:
            when(me < owners, all_home)


def exchange(slot_row, quadrature, start_state, up, down, rate):
    count, elems, nodes = rate.shape
    n = lax.axis_size("tm")
    rows = max(8, elems // n)
    q_high, q_low = split(np.kron(quadrature, np.eye(8)))
    piece = pltpu.VMEM((2, n, rows, nodes // 2), jnp.float32)
    whole = pltpu.VMEM((2, elems, nodes // 2), jnp.float32)
    face = pltpu.VMEM(up.shape, jnp.float32)
    vmem = pl.BlockSpec(memory_space=pltpu.VMEM)
    last_row = [float(x) for x in quadrature[-1].astype(np.float32)]
    return pl.pallas_call(
        functools.partial(exchange_kernel, last_row),
        out_shape=(
            jax.ShapeDtypeStruct((elems, nodes), jnp.float32),
            jax.ShapeDtypeStruct((count, 2 * up.shape[1], 128), jnp.float32),
            jax.ShapeDtypeStruct(rate.shape, jnp.float32),
        ),
        in_specs=[vmem] * 6 + [pl.BlockSpec(memory_space=pl.ANY)],
        out_specs=(vmem, vmem, vmem),
        scratch_shapes=[
            pltpu.VMEM(rate.shape, jnp.float32),
            face,
            face,
            whole,
            piece,
            piece,
            whole,
            pltpu.SemaphoreType.DMA,
            pltpu.SemaphoreType.DMA((2,)),
            pltpu.SemaphoreType.DMA((2,)),
        ]
        + [pltpu.SemaphoreType.DMA((2, n))] * 4,
        compiler_params=pltpu.CompilerParams(
            collective_id=0, has_side_effects=True, vmem_limit_bytes=32 * 2**20
        ),
        name="exchange",
    )(slot_row, q_high, q_low, start_state, up, down, rate)


def whole_block(*shape):
    return pl.BlockSpec(shape, lambda i: (0,) * len(shape))


def cost(flops, moved):
    return pl.CostEstimate(flops=flops, bytes_accessed=moved, transcendentals=0)


def on_device(iterate, start_state, mobility, slot_element):
    values = iterate[0]
    count, elems, nodes = values.shape
    stiffness, weights, quadrature = spectral_tables(count)
    k_high, k_low = split(stiffness)
    factor = flux_factor(weights)
    end_ratio = float((weights[0] + weights[-1]) / weights[0])
    slot_row = slot_element.reshape(1, elems)
    half = elems // 4
    f32 = jnp.float32
    params = pltpu.CompilerParams(vmem_limit_bytes=24 * 2**20)
    field = jax.ShapeDtypeStruct((count, elems, nodes), f32)
    face_shape = jax.ShapeDtypeStruct((count, half, 128), f32)
    times = pl.BlockSpec((T_BLOCK, elems, nodes), lambda i: (i, 0, 0))
    face_times = pl.BlockSpec((T_BLOCK, half, 128), lambda i: (i, 0, 0))
    size = count * elems * nodes
    rate, up, down = pl.pallas_call(
        functools.partial(flux_kernel, end_ratio),
        out_shape=(field, face_shape, face_shape),
        grid=(count // T_BLOCK,),
        in_specs=[
            whole_block(1, elems),
            whole_block(1, elems),
            times,
            whole_block(nodes, nodes),
            whole_block(nodes, nodes),
            whole_block(elems, nodes),
        ],
        out_specs=(times, face_times, face_times),
        compiler_params=pltpu.CompilerParams(vmem_limit_bytes=60 * 2**20),
        cost_estimate=cost(6 * size * nodes, 8 * size),
        name="flux",
    )(slot_row, mobility.reshape(1, elems), values, k_high, k_low, factor)
    base, faces, integral = exchange(slot_row, quadrature, start_state, up, down, rate)
    result = pl.pallas_call(
        final_kernel,
        out_shape=field,
        grid=(count // T_BLOCK,),
        in_specs=[
            whole_block(1, elems),
            whole_block(elems, nodes),
            pl.BlockSpec((T_BLOCK, 2 * half, 128), lambda i: (i, 0, 0)),
            times,
        ],
        out_specs=times,
        compiler_params=params,
        name="final",
    )(slot_row, base, faces, integral)
    return result[None]


def solution(mesh):
    in_specs = (P("tm", None, "space", None), P("space", None), P("space"), P("space", None))
    out_specs = P("tm", None, "space", None)
    return jax.shard_map(
        on_device, mesh=mesh, in_specs=in_specs, out_specs=out_specs, check_vma=False
    )
```

```python
import functools

import jax
import jax.numpy as jnp
import ml_dtypes
import numpy as np
from jax import lax
from jax.experimental import pallas as pl
from jax.experimental.pallas import tpu as pltpu
from jax.sharding import PartitionSpec as P

EX = 8
EY = 8
EZ_DEV = 2
NODES = 512


REACTION_RATE = 4.0
DIFFUSIVITY = 0.002
SEGMENT_SPAN = 0.1
T_BLOCK = 4
ROLL = pltpu.roll


def legendre_rows(points, order_n):
    table = np.zeros((points.shape[0], order_n + 1))
    table[:, 0] = 1.0
    table[:, 1] = points
    for k in range(2, order_n + 1):
        table[:, k] = ((2 * k - 1) * points * table[:, k - 1] - (k - 1) * table[:, k - 2]) / k
    return table


def spectral_tables(time_count):
    order_n = 7
    points = -np.cos(np.pi * np.arange(order_n + 1) / order_n)
    for _ in range(60):
        legendre = legendre_rows(points, order_n)
        points = points - (points * legendre[:, order_n] - legendre[:, order_n - 1]) / (
            (order_n + 1) * legendre[:, order_n]
        )
    legendre = legendre_rows(points, order_n)
    top_poly = legendre[:, order_n]
    weights = 2.0 / (order_n * (order_n + 1) * top_poly**2)
    derivative = np.zeros((order_n + 1, order_n + 1))
    for i in range(order_n + 1):
        for j in range(order_n + 1):
            if i != j:
                derivative[i, j] = top_poly[i] / (top_poly[j] * (points[i] - points[j]))
    derivative[0, 0] = -order_n * (order_n + 1) / 4.0
    derivative[order_n, order_n] = order_n * (order_n + 1) / 4.0
    stiff_1d = derivative.T @ (weights[:, None] * derivative)
    mass_1d = np.zeros((order_n + 1, order_n + 1))
    mass_1d[np.arange(order_n + 1), np.arange(order_n + 1)] = weights
    stiffness = 0.5 * (
        np.kron(np.kron(stiff_1d, mass_1d), mass_1d)
        + np.kron(np.kron(mass_1d, stiff_1d), mass_1d)
        + np.kron(np.kron(mass_1d, mass_1d), stiff_1d)
    )
    angles = np.pi - np.pi * np.arange(time_count) / (time_count - 1)
    cheb_nodes = np.cos(angles)
    vandermonde = np.cos(np.outer(angles, np.arange(time_count)))
    degree = time_count - 1
    half_ends = np.ones(time_count)
    half_ends[0] = 0.5
    half_ends[degree] = 0.5
    inverse_v = 2.0 / degree * vandermonde.T * half_ends[None, :] * half_ends[:, None]
    integral_table = np.zeros((time_count, time_count))
    integral_table[:, 0] = cheb_nodes + 1.0
    integral_table[:, 1] = 0.5 * (cheb_nodes**2 - 1.0)
    for n in range(2, time_count):
        upper_term = np.cos((n + 1) * angles) / (n + 1) - np.cos((n - 1) * angles) / (n - 1)
        lower_term = (-1.0) ** (n + 1) / (n + 1) - (-1.0) ** (n - 1) / (n - 1)
        integral_table[:, n] = 0.5 * (upper_term - lower_term)
    quadrature = 0.5 * SEGMENT_SPAN * integral_table @ inverse_v
    return stiffness, weights, quadrature


def split(table):
    high = table.astype(ml_dtypes.bfloat16)
    return high, (table - high.astype(np.float64)).astype(ml_dtypes.bfloat16)


def halves(value):
    high = value.astype(jnp.bfloat16)
    return high, (value - high.astype(jnp.float32)).astype(jnp.bfloat16)


def mm(a, b):
    return jnp.dot(a, b, preferred_element_type=jnp.float32)


def mm3(a, b):
    return mm(a[0], b[0]) + (mm(a[1], b[0]) + mm(a[0], b[1]))


def flux_factor(weights):
    def assembled(count, ends):
        table = np.tile(weights, (count, 1))
        shared = weights[0] + weights[-1]
        table[1:, 0] = shared
        table[:-1, -1] = shared
        if not ends:
            table[0, 0] = shared
            table[-1, -1] = shared
        return table

    z, y, x = assembled(EZ_DEV, False), assembled(EY, True), assembled(EX, True)
    mass = 0.125 * np.einsum("ai,bj,ck->abcijk", z, y, x)
    return (-DIFFUSIVITY / mass).reshape(EZ_DEV * EY * EX, NODES).astype(np.float32)


def column(row, mask):
    return jnp.sum(jnp.where(mask, row.astype(jnp.float32), 0.0), axis=1, keepdims=True)


def slots_as_column(slot_row):
    square = (slot_row.shape[1], slot_row.shape[1])
    same = lax.broadcasted_iota(jnp.int32, square, 0) == lax.broadcasted_iota(jnp.int32, square, 1)
    return column(slot_row[...], same).astype(jnp.int32)


def one_hot(mask):
    return mask.astype(jnp.float32).astype(jnp.bfloat16)


def flux_setup(slot_row, mobility):
    square = (slot_row.shape[1], slot_row.shape[1])
    place = slot_row[...] == lax.broadcasted_iota(jnp.int32, square, 0)
    to_store = one_hot(slots_as_column(slot_row) == lax.broadcasted_iota(jnp.int32, square, 1))
    return column(mobility[...], place), one_hot(place), to_store


def flux_block(end_ratio, setup, values, k_high, k_low, factor, rate, up, down):
    natural_mobility, to_natural, to_store = setup
    count, elems = values.shape[0], values.shape[1]
    layer = elems // 2
    position = lax.axis_index("space")
    low_end = jnp.where(position == 0, end_ratio, 1.0).astype(jnp.float32)
    high_end = jnp.where(position == lax.axis_size("space") - 1, end_ratio, 1.0).astype(jnp.float32)
    rows = []
    for t in range(count):
        scaled = halves(values[t])
        rows.append([mm(to_natural, part).astype(jnp.bfloat16) for part in scaled])
    natural = [jnp.concatenate([row[i] for row in rows], axis=0) for i in range(2)]
    flux = mm3(natural, (k_high[...], k_low[...]))

    cube = (elems // 8, 8, 128)
    lane = lax.broadcasted_iota(jnp.int32, cube, 2)
    ex = lax.broadcasted_iota(jnp.int32, cube, 1)
    ey = lax.broadcasted_iota(jnp.int32, cube, 0) % 8
    kx, ky = lane % 8, lane // 8 % 8
    x_next, x_prev = (kx == 7) & (ex < 7), (kx == 0) & (ex > 0)
    y_next, y_prev = (ky == 7) & (ey < 7), (ky == 0) & (ey > 0)
    left = lax.broadcasted_iota(jnp.int32, (layer, 128), 1) < 64
    left_half = lax.broadcasted_iota(jnp.int32, (layer // 2, 128), 1) < 64
    for t in range(count):
        columns = []
        for c in range(4):
            f = flux[t * elems : (t + 1) * elems, c * 128 : (c + 1) * 128]
            f = (f * natural_mobility).reshape(cube)
            f = (
                f
                + jnp.where(x_next, ROLL(ROLL(f, 7, 2), 7, 1), 0.0)
                + jnp.where(x_prev, ROLL(ROLL(f, 121, 2), 1, 1), 0.0)
            )
            after, before = ROLL(f, 56, 2), ROLL(f, 72, 2)
            after = jnp.concatenate([after[1:], after[:1]], axis=0)
            before = jnp.concatenate([before[-1:], before[:-1]], axis=0)
            f = f + jnp.where(y_next, after, 0.0) + jnp.where(y_prev, before, 0.0)
            columns.append(f.reshape(elems, 128) * factor[:, c * 128 : (c + 1) * 128])
        first, last = columns[0], columns[3]
        bottom, top = first[:layer], last[layer:]
        half = layer // 2
        up[t] = jnp.where(left_half, ROLL(top[:half], 64, 1), top[half:])
        down[t] = jnp.where(left_half, bottom[half:], ROLL(bottom[:half], 64, 1))
        first_top = first[layer:] + jnp.where(left, ROLL(last[:layer], 64, 1), 0.0)
        last_bottom = last[:layer] + jnp.where(left, 0.0, ROLL(first[layer:], 64, 1))
        columns[0] = jnp.concatenate([jnp.where(left, bottom * low_end, bottom), first_top], axis=0)
        columns[3] = jnp.concatenate([last_bottom, jnp.where(left, top, top * high_end)], axis=0)
        high, low = halves(jnp.concatenate(columns, axis=1))
        stored = mm(to_store, high) + mm(to_store, low)
        v = values[t]
        rate[t] = REACTION_RATE * (v - v * v * v) + stored


def store_face(slots, face):
    layer = face.shape[0]
    elem = lax.broadcasted_iota(jnp.int32, (2 * layer, layer), 1)
    high, low = halves(face)
    columns = []
    for first in (0, layer):
        pick = one_hot(slots == elem + first)
        columns.append(mm(pick, high) + mm(pick, low))
    left = lax.broadcasted_iota(jnp.int32, columns[0].shape, 1) < 64
    return jnp.where(left, columns[0], 0.0), jnp.where(left, 0.0, columns[1])


def final_kernel(slot_row, base, faces, integral, out):
    slots = slots_as_column(slot_row)
    for t in range(integral.shape[0]):
        first, last = store_face(slots, faces[t])
        whole = base[...] + integral[t]
        out[t, :, :128] = whole[:, :128] + first
        out[t, :, 128:384] = whole[:, 128:384]
        out[t, :, 384:] = whole[:, 384:] + last


def exchange_kernel(
    last_row, end_ratio, slot_row, mobility, q_high, q_low, start, *refs
):
    (
    values, k_high, k_low, factor, base, faces, integral_out,
    values_v, k_high_v, k_low_v, factor_v, up, down, integral, held, below, above, increment, arrived, sums, earlier,
    loaded, tables, stored, face_sent, face_got, sent, got, returned, back,
    ) = refs
    n, me = lax.axis_size("tm"), lax.axis_index("tm")
    extent, position = lax.axis_size("space"), lax.axis_index("space")
    count, elems, nodes = held.shape
    rows = arrived.shape[2]
    owners = elems // rows
    mesh_id = pl.DeviceIdType.MESH

    def piece(ref, part, j):
        return ref.at[part, pl.ds(pl.multiple_of(j * rows, 8), rows), :]

    def outward(part, j, source):
        return pltpu.make_async_remote_copy(
            src_ref=piece(increment, part, j),
            dst_ref=arrived.at[part, source],
            send_sem=sent.at[part, j],
            recv_sem=got.at[part, source],
            device_id={"tm": j},
            device_id_type=mesh_id,
        )

    def homeward(part, j, owner):
        return pltpu.make_async_remote_copy(
            src_ref=sums.at[part, j],
            dst_ref=piece(earlier, part, owner),
            send_sem=returned.at[part, j],
            recv_sem=back.at[part, owner],
            device_id={"tm": j},
            device_id_type=mesh_id,
        )

    def face_copy(source, target, which, step):
        return pltpu.make_async_remote_copy(
            src_ref=source,
            dst_ref=target,
            send_sem=face_sent.at[which],
            recv_sem=face_got.at[which],
            device_id={"space": position + step},
            device_id_type=mesh_id,
        )

    def others(action):
        def one(d, carry):
            action(lax.rem(me + d, n))
            return carry

        lax.fori_loop(1, n, one, 0)

    def when(condition, action):
        pl.when(condition)(action)

    def other_owners(action):
        if owners == n:
            others(action)
        else:
            others(lambda j: when(j < owners, lambda: action(j)))

    def send_increment(part):
        @pl.when(me < n - 1)
        def _():
            other_owners(lambda j: outward(part, j, me).start())

    def scan(part):
        def hand_out(i, running):
            @pl.when(i != me)
            def _():
                sums[part, i] = running
                homeward(part, i, me).start()

            @pl.when(i == me)
            def _():
                piece(earlier, part, me)[...] = running

        def add(i, running):
            @pl.when(i != me)
            def _():
                outward(part, i, i).wait_recv()

            @pl.when(i == me)
            def _():
                arrived[part, i] = piece(increment, part, me)[...]

            running = running + arrived[part, i]
            hand_out(i + 1, running)
            return running

        def own():
            lax.fori_loop(0, n - 1, add, jnp.zeros(arrived.shape[2:], jnp.float32))

        if owners == n:
            own()
        else:
            when(me < owners, own)

    def load(block):
        these = pl.ds(block * T_BLOCK, T_BLOCK)
        return pltpu.make_async_copy(values.at[these], values_v.at[these], loaded.at[block])

    table_copies = [
        pltpu.make_async_copy(source, target, tables.at[k])
        for k, (source, target) in enumerate(
            ((k_high, k_high_v), (k_low, k_low_v), (factor, factor_v))
        )
    ]
    load(0).start()
    for copy in table_copies:
        copy.start()
    for block in range(1, count // T_BLOCK):
        load(block).start()
    barrier = pltpu.get_barrier_semaphore()

    def greet(device):
        pl.semaphore_signal(barrier, inc=1, device_id=device, device_id_type=mesh_id)

    others(lambda j: greet({"tm": j}))
    has_below, has_above = position > 0, position < extent - 1
    when(has_below, lambda: greet({"space": position - 1}))
    when(has_above, lambda: greet({"space": position + 1}))

    setup = flux_setup(slot_row, mobility)
    for copy in table_copies:
        copy.wait()

    def flux(block, carry):
        load(block).wait()
        these = pl.ds(block * T_BLOCK, T_BLOCK)
        flux_block(
            end_ratio, setup, values_v.at[these], k_high_v, k_low_v, factor_v,
            held.at[these], up.at[these], down.at[these],
        )
        return carry

    lax.fori_loop(0, count // T_BLOCK, flux, 0)
    pl.semaphore_wait(barrier, n - 1 + has_below.astype(jnp.int32) + has_above.astype(jnp.int32))

    when(has_above, lambda: face_copy(up, below, 0, 1).start())
    when(has_below, lambda: face_copy(down, above, 1, -1).start())
    total = last_row[0] * held[0, :, 128:384]
    for t in range(1, count):
        total = total + last_row[t] * held[t, :, 128:384]
    increment[0] = total
    send_increment(0)

    width = 32

    def store(index):
        these = pl.ds(pl.multiple_of(index * width, 8), width)
        return pltpu.make_async_copy(
            integral.at[:, these, :], integral_out.at[:, these, :], stored.at[index]
        )

    def quadrature(index, carry):
        for k in range(width // 8):
            these = pl.ds(pl.multiple_of(index * width + k * 8, 8), 8)
            part = held[:, these, :].reshape(count * 8, nodes)
            done = mm3((q_high[...], q_low[...]), halves(part))
            integral[:, these, :] = done.reshape(count, 8, nodes)
        store(index).start()
        return carry

    lax.fori_loop(0, elems // width, quadrature, 0)

    @pl.when(has_below)
    def _():
        face_copy(up, below, 0, 1).wait_recv()

    @pl.when(position == 0)
    def _():
        below[...] = jnp.zeros_like(below)

    @pl.when(has_above)
    def _():
        face_copy(down, above, 1, -1).wait_recv()

    @pl.when(position == extent - 1)
    def _():
        above[...] = jnp.zeros_like(above)

    left = lax.broadcasted_iota(jnp.int32, below.shape, 2) < 64
    lower, upper = below[...], above[...]
    face = jnp.concatenate(
        [
            jnp.where(left, lower, upper),
            jnp.where(left, ROLL(lower, 64, 2), ROLL(upper, 64, 2)),
        ],
        axis=1,
    )
    for block in range(face.shape[1] // 8):
        part = face[:, block * 8 : block * 8 + 8, :].reshape(count * 8, 128)
        done = mm3((q_high[...], q_low[...]), halves(part))
        faces[:, block * 8 : block * 8 + 8, :] = done.reshape(count, 8, 128)
    first, last = store_face(slots_as_column(slot_row), faces[count - 1])
    increment[1, :, :128] = integral[count - 1, :, :128] + first
    increment[1, :, 128:] = integral[count - 1, :, 384:] + last
    send_increment(1)
    scan(0)
    scan(1)

    @pl.when(me == 0)
    def _():
        base[...] = start[...]

    @pl.when(me > 0)
    def _():
        for part in range(2):
            other_owners(lambda j: homeward(part, j, j).wait_recv())
        base[:, :128] = start[:, :128] + earlier[1, :, :128]
        base[:, 128:384] = start[:, 128:384] + earlier[0]
        base[:, 384:] = start[:, 384:] + earlier[1, :, 128:]

    for index in range(elems // width):
        store(index).wait()
    when(has_above, lambda: face_copy(up, below, 0, 1).wait_send())
    when(has_below, lambda: face_copy(down, above, 1, -1).wait_send())

    def sent_home(part, j):
        when(j > 0, lambda: homeward(part, j, me).wait_send())

    for part in range(2):

        @pl.when(me < n - 1)
        def _():
            other_owners(lambda j: outward(part, j, me).wait_send())

        def all_home():
            others(lambda j: sent_home(part, j))

        if owners == n:
            all_home()
        else:
            when(me < owners, all_home)


def exchange(end_ratio, slot_row, mobility, quadrature, start_state, values, tables):
    count, elems, nodes = values.shape
    n = lax.axis_size("tm")
    rows = max(8, elems // n)
    q_high, q_low = split(np.kron(quadrature, np.eye(8)))
    f32 = jnp.float32
    piece = pltpu.VMEM((2, n, rows, nodes // 2), f32)
    whole = pltpu.VMEM((2, elems, nodes // 2), f32)
    face = pltpu.VMEM((count, elems // 4, 128), f32)
    field = pltpu.VMEM(values.shape, f32)
    vmem = pl.BlockSpec(memory_space=pltpu.VMEM)
    anywhere = pl.BlockSpec(memory_space=pl.ANY)
    dma = pltpu.SemaphoreType.DMA
    last_row = [float(x) for x in quadrature[-1].astype(np.float32)]
    return pl.pallas_call(
        functools.partial(exchange_kernel, last_row, end_ratio),
        out_shape=(
            jax.ShapeDtypeStruct((elems, nodes), f32),
            jax.ShapeDtypeStruct((count, elems // 2, 128), f32),
            jax.ShapeDtypeStruct(values.shape, f32),
        ),
        in_specs=[vmem] * 5 + [anywhere] * 4,
        out_specs=(vmem, vmem, anywhere),
        scratch_shapes=[
            field,
            pltpu.VMEM((nodes, nodes), jnp.bfloat16),
            pltpu.VMEM((nodes, nodes), jnp.bfloat16),
            pltpu.VMEM((elems, nodes), f32),
            face,
            face,
            field,
            field,
            face,
            face,
            whole,
            piece,
            piece,
            whole,
            dma((count // T_BLOCK,)),
            dma((3,)),
            dma((elems // 32,)),
            dma((2,)),
            dma((2,)),
        ]
        + [dma((2, n))] * 4,
        compiler_params=pltpu.CompilerParams(
            collective_id=0, has_side_effects=True, vmem_limit_bytes=60 * 2**20
        ),
        name="exchange",
    )(slot_row, mobility, q_high, q_low, start_state, values, *tables)


def whole_block(*shape):
    return pl.BlockSpec(shape, lambda i: (0,) * len(shape))


def on_device(iterate, start_state, mobility, slot_element):
    values = iterate[0]
    count, elems, nodes = values.shape
    stiffness, weights, quadrature = spectral_tables(count)
    k_high, k_low = split(stiffness)
    factor = flux_factor(weights)
    end_ratio = float((weights[0] + weights[-1]) / weights[0])
    slot_row = slot_element.reshape(1, elems)
    half = elems // 4
    params = pltpu.CompilerParams(vmem_limit_bytes=60 * 2**20)
    field = jax.ShapeDtypeStruct((count, elems, nodes), jnp.float32)
    times = pl.BlockSpec((T_BLOCK, elems, nodes), lambda i: (i, 0, 0))
    base, faces, integral = exchange(
        end_ratio,
        slot_row,
        mobility.reshape(1, elems),
        quadrature,
        start_state,
        values,
        (k_high, k_low, factor),
    )
    result = pl.pallas_call(
        final_kernel,
        out_shape=field,
        grid=(count // T_BLOCK,),
        in_specs=[
            whole_block(1, elems),
            whole_block(elems, nodes),
            pl.BlockSpec((T_BLOCK, 2 * half, 128), lambda i: (i, 0, 0)),
            times,
        ],
        out_specs=times,
        compiler_params=params,
        name="final",
    )(slot_row, base, faces, integral)
    return result[None]


def solution(mesh):
    in_specs = (P("tm", None, "space", None), P("space", None), P("space"), P("space", None))
    out_specs = P("tm", None, "space", None)
    return jax.shard_map(
        on_device, mesh=mesh, in_specs=in_specs, out_specs=out_specs, check_vma=False
    )
```

```python
import functools

import jax
import jax.numpy as jnp
import ml_dtypes
import numpy as np
from jax import lax
from jax.experimental import pallas as pl
from jax.experimental.pallas import tpu as pltpu
from jax.sharding import PartitionSpec as P

EX = 8
EY = 8
EZ_DEV = 2
NODES = 512


REACTION_RATE = 4.0
DIFFUSIVITY = 0.002
SEGMENT_SPAN = 0.1
T_BLOCK = 4
FINAL_BLOCK = 2
ROLL = pltpu.roll


def legendre_rows(points, order_n):
    table = np.zeros((points.shape[0], order_n + 1))
    table[:, 0] = 1.0
    table[:, 1] = points
    for k in range(2, order_n + 1):
        table[:, k] = ((2 * k - 1) * points * table[:, k - 1] - (k - 1) * table[:, k - 2]) / k
    return table


def spectral_tables(time_count):
    order_n = 7
    points = -np.cos(np.pi * np.arange(order_n + 1) / order_n)
    for _ in range(60):
        legendre = legendre_rows(points, order_n)
        points = points - (points * legendre[:, order_n] - legendre[:, order_n - 1]) / (
            (order_n + 1) * legendre[:, order_n]
        )
    legendre = legendre_rows(points, order_n)
    top_poly = legendre[:, order_n]
    weights = 2.0 / (order_n * (order_n + 1) * top_poly**2)
    derivative = np.zeros((order_n + 1, order_n + 1))
    for i in range(order_n + 1):
        for j in range(order_n + 1):
            if i != j:
                derivative[i, j] = top_poly[i] / (top_poly[j] * (points[i] - points[j]))
    derivative[0, 0] = -order_n * (order_n + 1) / 4.0
    derivative[order_n, order_n] = order_n * (order_n + 1) / 4.0
    stiff_1d = derivative.T @ (weights[:, None] * derivative)
    mass_1d = np.zeros((order_n + 1, order_n + 1))
    mass_1d[np.arange(order_n + 1), np.arange(order_n + 1)] = weights
    stiffness = 0.5 * (
        np.kron(np.kron(stiff_1d, mass_1d), mass_1d)
        + np.kron(np.kron(mass_1d, stiff_1d), mass_1d)
        + np.kron(np.kron(mass_1d, mass_1d), stiff_1d)
    )
    angles = np.pi - np.pi * np.arange(time_count) / (time_count - 1)
    cheb_nodes = np.cos(angles)
    vandermonde = np.cos(np.outer(angles, np.arange(time_count)))
    degree = time_count - 1
    half_ends = np.ones(time_count)
    half_ends[0] = 0.5
    half_ends[degree] = 0.5
    inverse_v = 2.0 / degree * vandermonde.T * half_ends[None, :] * half_ends[:, None]
    integral_table = np.zeros((time_count, time_count))
    integral_table[:, 0] = cheb_nodes + 1.0
    integral_table[:, 1] = 0.5 * (cheb_nodes**2 - 1.0)
    for n in range(2, time_count):
        upper_term = np.cos((n + 1) * angles) / (n + 1) - np.cos((n - 1) * angles) / (n - 1)
        lower_term = (-1.0) ** (n + 1) / (n + 1) - (-1.0) ** (n - 1) / (n - 1)
        integral_table[:, n] = 0.5 * (upper_term - lower_term)
    quadrature = 0.5 * SEGMENT_SPAN * integral_table @ inverse_v
    return stiffness, weights, quadrature


def split(table):
    high = table.astype(ml_dtypes.bfloat16)
    return high, (table - high.astype(np.float64)).astype(ml_dtypes.bfloat16)


def halves(value):
    high = value.astype(jnp.bfloat16)
    return high, (value - high.astype(jnp.float32)).astype(jnp.bfloat16)


def mm(a, b):
    return jnp.dot(a, b, preferred_element_type=jnp.float32)


def mm3(a, b):
    return mm(a[0], b[0]) + (mm(a[1], b[0]) + mm(a[0], b[1]))


def flux_factor(weights):
    def assembled(count, ends):
        table = np.tile(weights, (count, 1))
        shared = weights[0] + weights[-1]
        table[1:, 0] = shared
        table[:-1, -1] = shared
        if not ends:
            table[0, 0] = shared
            table[-1, -1] = shared
        return table

    z, y, x = assembled(EZ_DEV, False), assembled(EY, True), assembled(EX, True)
    mass = 0.125 * np.einsum("ai,bj,ck->abcijk", z, y, x)
    return (-DIFFUSIVITY / mass).reshape(EZ_DEV * EY * EX, NODES).astype(np.float32)


def column(row, mask):
    return jnp.sum(jnp.where(mask, row.astype(jnp.float32), 0.0), axis=1, keepdims=True)


def slots_as_column(slot_row):
    square = (slot_row.shape[1], slot_row.shape[1])
    same = lax.broadcasted_iota(jnp.int32, square, 0) == lax.broadcasted_iota(jnp.int32, square, 1)
    return column(slot_row[...], same).astype(jnp.int32)


def one_hot(mask):
    return mask.astype(jnp.float32).astype(jnp.bfloat16)


def flux_setup(slot_row, mobility):
    square = (slot_row.shape[1], slot_row.shape[1])
    place = slot_row[...] == lax.broadcasted_iota(jnp.int32, square, 0)
    to_store = one_hot(slots_as_column(slot_row) == lax.broadcasted_iota(jnp.int32, square, 1))
    return column(mobility[...], place), one_hot(place), to_store


def flux_block(end_ratio, setup, values, k_high, k_low, factor, rate, up, down):
    natural_mobility, to_natural, to_store = setup
    count, elems = values.shape[0], values.shape[1]
    layer = elems // 2
    position = lax.axis_index("space")
    low_end = jnp.where(position == 0, end_ratio, 1.0).astype(jnp.float32)
    high_end = jnp.where(position == lax.axis_size("space") - 1, end_ratio, 1.0).astype(jnp.float32)
    rows = []
    for t in range(count):
        scaled = halves(values[t])
        rows.append([mm(to_natural, part).astype(jnp.bfloat16) for part in scaled])
    natural = [jnp.concatenate([row[i] for row in rows], axis=0) for i in range(2)]
    flux = mm3(natural, (k_high[...], k_low[...]))

    cube = (elems // 8, 8, 128)
    lane = lax.broadcasted_iota(jnp.int32, cube, 2)
    ex = lax.broadcasted_iota(jnp.int32, cube, 1)
    ey = lax.broadcasted_iota(jnp.int32, cube, 0) % 8
    kx, ky = lane % 8, lane // 8 % 8
    x_next, x_prev = (kx == 7) & (ex < 7), (kx == 0) & (ex > 0)
    y_next, y_prev = (ky == 7) & (ey < 7), (ky == 0) & (ey > 0)
    left = lax.broadcasted_iota(jnp.int32, (layer, 128), 1) < 64
    left_half = lax.broadcasted_iota(jnp.int32, (layer // 2, 128), 1) < 64
    for t in range(count):
        columns = []
        for c in range(4):
            f = flux[t * elems : (t + 1) * elems, c * 128 : (c + 1) * 128]
            f = (f * natural_mobility).reshape(cube)
            f = (
                f
                + jnp.where(x_next, ROLL(ROLL(f, 7, 2), 7, 1), 0.0)
                + jnp.where(x_prev, ROLL(ROLL(f, 121, 2), 1, 1), 0.0)
            )
            after, before = ROLL(f, 56, 2), ROLL(f, 72, 2)
            after = jnp.concatenate([after[1:], after[:1]], axis=0)
            before = jnp.concatenate([before[-1:], before[:-1]], axis=0)
            f = f + jnp.where(y_next, after, 0.0) + jnp.where(y_prev, before, 0.0)
            columns.append(f.reshape(elems, 128) * factor[:, c * 128 : (c + 1) * 128])
        first, last = columns[0], columns[3]
        bottom, top = first[:layer], last[layer:]
        half = layer // 2
        up[t] = jnp.where(left_half, ROLL(top[:half], 64, 1), top[half:])
        down[t] = jnp.where(left_half, bottom[half:], ROLL(bottom[:half], 64, 1))
        first_top = first[layer:] + jnp.where(left, ROLL(last[:layer], 64, 1), 0.0)
        last_bottom = last[:layer] + jnp.where(left, 0.0, ROLL(first[layer:], 64, 1))
        columns[0] = jnp.concatenate([jnp.where(left, bottom * low_end, bottom), first_top], axis=0)
        columns[3] = jnp.concatenate([last_bottom, jnp.where(left, top, top * high_end)], axis=0)
        high, low = halves(jnp.concatenate(columns, axis=1))
        stored = mm(to_store, high) + mm(to_store, low)
        v = values[t]
        rate[t] = REACTION_RATE * (v - v * v * v) + stored


def store_face(slots, face):
    layer = face.shape[0]
    elem = lax.broadcasted_iota(jnp.int32, (2 * layer, layer), 1)
    high, low = halves(face)
    columns = []
    for first in (0, layer):
        pick = one_hot(slots == elem + first)
        columns.append(mm(pick, high) + mm(pick, low))
    left = lax.broadcasted_iota(jnp.int32, columns[0].shape, 1) < 64
    return jnp.where(left, columns[0], 0.0), jnp.where(left, 0.0, columns[1])


def final_kernel(slot_row, base, faces, integral, out):
    slots = slots_as_column(slot_row)
    for t in range(integral.shape[0]):
        first, last = store_face(slots, faces[t])
        whole = base[...] + integral[t]
        out[t, :, :128] = whole[:, :128] + first
        out[t, :, 128:384] = whole[:, 128:384]
        out[t, :, 384:] = whole[:, 384:] + last


def exchange_kernel(
    last_row, end_ratio, slot_row, mobility, q_high, q_low, start, *refs
):
    (
    values, k_high, k_low, factor, base, faces, integral_out,
    values_v, k_high_v, k_low_v, factor_v, up, down, integral, held, below, above, increment, arrived, sums, earlier,
    loaded, tables, stored, face_sent, face_got, sent, got, returned, back,
    ) = refs
    n, me = lax.axis_size("tm"), lax.axis_index("tm")
    extent, position = lax.axis_size("space"), lax.axis_index("space")
    count, elems, nodes = held.shape
    rows = arrived.shape[2]
    owners = elems // rows
    mesh_id = pl.DeviceIdType.MESH

    def piece(ref, part, j):
        return ref.at[part, pl.ds(pl.multiple_of(j * rows, 8), rows), :]

    def outward(part, j, source):
        return pltpu.make_async_remote_copy(
            src_ref=piece(increment, part, j),
            dst_ref=arrived.at[part, source],
            send_sem=sent.at[part, j],
            recv_sem=got.at[part, source],
            device_id={"tm": j},
            device_id_type=mesh_id,
        )

    def homeward(part, j, owner):
        return pltpu.make_async_remote_copy(
            src_ref=sums.at[part, j],
            dst_ref=piece(earlier, part, owner),
            send_sem=returned.at[part, j],
            recv_sem=back.at[part, owner],
            device_id={"tm": j},
            device_id_type=mesh_id,
        )

    def face_copy(which, block):
        source, target, step = ((up, below, 1), (down, above, -1))[which]
        these = pl.ds(block * T_BLOCK, T_BLOCK)
        return pltpu.make_async_remote_copy(
            src_ref=source.at[these],
            dst_ref=target.at[these],
            send_sem=face_sent.at[which, block],
            recv_sem=face_got.at[which, block],
            device_id={"space": position + step},
            device_id_type=mesh_id,
        )

    def others(action):
        def one(d, carry):
            action(lax.rem(me + d, n))
            return carry

        lax.fori_loop(1, n, one, 0)

    def when(condition, action):
        pl.when(condition)(action)

    def other_owners(action):
        if owners == n:
            others(action)
        else:
            others(lambda j: when(j < owners, lambda: action(j)))

    def send_increment(part):
        @pl.when(me < n - 1)
        def _():
            other_owners(lambda j: outward(part, j, me).start())

    def scan(part):
        def hand_out(i, running):
            @pl.when(i != me)
            def _():
                sums[part, i] = running
                homeward(part, i, me).start()

            @pl.when(i == me)
            def _():
                piece(earlier, part, me)[...] = running

        def add(i, running):
            @pl.when(i != me)
            def _():
                outward(part, i, i).wait_recv()

            @pl.when(i == me)
            def _():
                arrived[part, i] = piece(increment, part, me)[...]

            running = running + arrived[part, i]
            hand_out(i + 1, running)
            return running

        def own():
            lax.fori_loop(0, n - 1, add, jnp.zeros(arrived.shape[2:], jnp.float32))

        if owners == n:
            own()
        else:
            when(me < owners, own)

    def load(block):
        these = pl.ds(block * T_BLOCK, T_BLOCK)
        return pltpu.make_async_copy(values.at[these], values_v.at[these], loaded.at[block])

    table_copies = [
        pltpu.make_async_copy(source, target, tables.at[k])
        for k, (source, target) in enumerate(
            ((k_high, k_high_v), (k_low, k_low_v), (factor, factor_v))
        )
    ]
    load(0).start()
    for copy in table_copies:
        copy.start()
    for block in range(1, count // T_BLOCK):
        load(block).start()
    barrier = pltpu.get_barrier_semaphore()

    def greet(device):
        pl.semaphore_signal(barrier, inc=1, device_id=device, device_id_type=mesh_id)

    others(lambda j: greet({"tm": j}))
    has_below, has_above = position > 0, position < extent - 1
    when(has_below, lambda: greet({"space": position - 1}))
    when(has_above, lambda: greet({"space": position + 1}))

    setup = flux_setup(slot_row, mobility)
    for copy in table_copies:
        copy.wait()

    def flux(block, carry):
        load(block).wait()
        these = pl.ds(block * T_BLOCK, T_BLOCK)
        flux_block(
            end_ratio, setup, values_v.at[these], k_high_v, k_low_v, factor_v,
            held.at[these], up.at[these], down.at[these],
        )

        @pl.when(block == 0)
        def _():
            nearby = has_below.astype(jnp.int32) + has_above.astype(jnp.int32)
            pl.semaphore_wait(barrier, n - 1 + nearby)

        when(has_above, lambda: face_copy(0, block).start())
        when(has_below, lambda: face_copy(1, block).start())
        return carry

    lax.fori_loop(0, count // T_BLOCK, flux, 0)
    blocks = range(count // T_BLOCK)

    def last_integral(ref, first, last):
        total = last_row[0] * ref[0, :, first:last]
        for t in range(1, count):
            total = total + last_row[t] * ref[t, :, first:last]
        return total

    increment[0] = last_integral(held, 128, 384)
    send_increment(0)

    width = 32

    def store(index):
        these = pl.ds(pl.multiple_of(index * width, 8), width)
        return pltpu.make_async_copy(
            integral.at[:, these, :], integral_out.at[:, these, :], stored.at[index]
        )

    def quadrature(index, carry):
        for k in range(width // 8):
            these = pl.ds(pl.multiple_of(index * width + k * 8, 8), 8)
            part = held[:, these, :].reshape(count * 8, nodes)
            done = mm3((q_high[...], q_low[...]), halves(part))
            integral[:, these, :] = done.reshape(count, 8, nodes)
        store(index).start()
        return carry

    pieces = elems // width
    lax.fori_loop(0, pieces // 2, quadrature, 0)
    outer = (last_integral(held, 0, 128), last_integral(held, 384, 512))

    @pl.when(has_below)
    def _():
        for block in blocks:
            face_copy(0, block).wait_recv()

    @pl.when(position == 0)
    def _():
        below[...] = jnp.zeros_like(below)

    @pl.when(has_above)
    def _():
        for block in blocks:
            face_copy(1, block).wait_recv()

    @pl.when(position == extent - 1)
    def _():
        above[...] = jnp.zeros_like(above)

    def unpacked(lower, upper):
        axis = lower.ndim - 1
        left = lax.broadcasted_iota(jnp.int32, lower.shape, axis) < 64
        near = jnp.where(left, lower, upper)
        far = jnp.where(left, ROLL(lower, 64, axis), ROLL(upper, 64, axis))
        return jnp.concatenate([near, far], axis=axis - 1)

    last_face = unpacked(last_integral(below, 0, 128), last_integral(above, 0, 128))
    first, last = store_face(slots_as_column(slot_row), last_face)
    increment[1, :, :128] = outer[0] + first
    increment[1, :, 128:] = outer[1] + last
    send_increment(1)
    scan(0)
    lax.fori_loop(pieces // 2, pieces, quadrature, 0)
    face = unpacked(below[...], above[...])
    for block in range(face.shape[1] // 8):
        part = face[:, block * 8 : block * 8 + 8, :].reshape(count * 8, 128)
        done = mm3((q_high[...], q_low[...]), halves(part))
        faces[:, block * 8 : block * 8 + 8, :] = done.reshape(count, 8, 128)
    scan(1)

    @pl.when(me == 0)
    def _():
        base[...] = start[...]

    @pl.when(me > 0)
    def _():
        for part in range(2):
            other_owners(lambda j: homeward(part, j, j).wait_recv())
        base[:, :128] = start[:, :128] + earlier[1, :, :128]
        base[:, 128:384] = start[:, 128:384] + earlier[0]
        base[:, 384:] = start[:, 384:] + earlier[1, :, 128:]

    for index in range(elems // width):
        store(index).wait()
    for block in blocks:
        when(has_above, lambda: face_copy(0, block).wait_send())
        when(has_below, lambda: face_copy(1, block).wait_send())

    def sent_home(part, j):
        when(j > 0, lambda: homeward(part, j, me).wait_send())

    for part in range(2):

        @pl.when(me < n - 1)
        def _():
            other_owners(lambda j: outward(part, j, me).wait_send())

        def all_home():
            others(lambda j: sent_home(part, j))

        if owners == n:
            all_home()
        else:
            when(me < owners, all_home)


def exchange(end_ratio, slot_row, mobility, quadrature, start_state, values, tables):
    count, elems, nodes = values.shape
    n = lax.axis_size("tm")
    rows = max(8, elems // n)
    q_high, q_low = split(np.kron(quadrature, np.eye(8)))
    f32 = jnp.float32
    piece = pltpu.VMEM((2, n, rows, nodes // 2), f32)
    whole = pltpu.VMEM((2, elems, nodes // 2), f32)
    face = pltpu.VMEM((count, elems // 4, 128), f32)
    field = pltpu.VMEM(values.shape, f32)
    vmem = pl.BlockSpec(memory_space=pltpu.VMEM)
    anywhere = pl.BlockSpec(memory_space=pl.ANY)
    dma = pltpu.SemaphoreType.DMA
    last_row = [float(x) for x in quadrature[-1].astype(np.float32)]
    return pl.pallas_call(
        functools.partial(exchange_kernel, last_row, end_ratio),
        out_shape=(
            jax.ShapeDtypeStruct((elems, nodes), f32),
            jax.ShapeDtypeStruct((count, elems // 2, 128), f32),
            jax.ShapeDtypeStruct(values.shape, f32),
        ),
        in_specs=[vmem] * 5 + [anywhere] * 4,
        out_specs=(vmem, vmem, anywhere),
        scratch_shapes=[
            field,
            pltpu.VMEM((nodes, nodes), jnp.bfloat16),
            pltpu.VMEM((nodes, nodes), jnp.bfloat16),
            pltpu.VMEM((elems, nodes), f32),
            face,
            face,
            field,
            field,
            face,
            face,
            whole,
            piece,
            piece,
            whole,
            dma((count // T_BLOCK,)),
            dma((3,)),
            dma((elems // 32,)),
            dma((2, count // T_BLOCK)),
            dma((2, count // T_BLOCK)),
        ]
        + [dma((2, n))] * 4,
        compiler_params=pltpu.CompilerParams(
            collective_id=0, has_side_effects=True, vmem_limit_bytes=60 * 2**20
        ),
        name="exchange",
    )(slot_row, mobility, q_high, q_low, start_state, values, *tables)


def whole_block(*shape):
    return pl.BlockSpec(shape, lambda i: (0,) * len(shape))


def on_device(iterate, start_state, mobility, slot_element):
    values = iterate[0]
    count, elems, nodes = values.shape
    stiffness, weights, quadrature = spectral_tables(count)
    k_high, k_low = split(stiffness)
    factor = flux_factor(weights)
    end_ratio = float((weights[0] + weights[-1]) / weights[0])
    slot_row = slot_element.reshape(1, elems)
    half = elems // 4
    params = pltpu.CompilerParams(vmem_limit_bytes=60 * 2**20)
    field = jax.ShapeDtypeStruct((count, elems, nodes), jnp.float32)
    times = pl.BlockSpec((FINAL_BLOCK, elems, nodes), lambda i: (i, 0, 0))
    base, faces, integral = exchange(
        end_ratio,
        slot_row,
        mobility.reshape(1, elems),
        quadrature,
        start_state,
        values,
        (k_high, k_low, factor),
    )
    result = pl.pallas_call(
        final_kernel,
        out_shape=field,
        grid=(count // FINAL_BLOCK,),
        in_specs=[
            whole_block(1, elems),
            whole_block(elems, nodes),
            pl.BlockSpec((FINAL_BLOCK, 2 * half, 128), lambda i: (i, 0, 0)),
            times,
        ],
        out_specs=times,
        compiler_params=params,
        name="final",
    )(slot_row, base, faces, integral)
    return result[None]


def solution(mesh):
    in_specs = (P("tm", None, "space", None), P("space", None), P("space"), P("space", None))
    out_specs = P("tm", None, "space", None)
    return jax.shard_map(
        on_device, mesh=mesh, in_specs=in_specs, out_specs=out_specs, check_vma=False
    )
```

```python
import functools

import jax
import jax.numpy as jnp
import ml_dtypes
import numpy as np
from jax import lax
from jax.experimental import pallas as pl
from jax.experimental.pallas import tpu as pltpu
from jax.sharding import PartitionSpec as P

EX = 8
EY = 8
EZ_DEV = 2
NODES = 512


REACTION_RATE = 4.0
DIFFUSIVITY = 0.002
SEGMENT_SPAN = 0.1
T_BLOCK = 4
FINAL_BLOCK = 4
ROLL = pltpu.roll


def legendre_rows(points, order_n):
    table = np.zeros((points.shape[0], order_n + 1))
    table[:, 0] = 1.0
    table[:, 1] = points
    for k in range(2, order_n + 1):
        table[:, k] = ((2 * k - 1) * points * table[:, k - 1] - (k - 1) * table[:, k - 2]) / k
    return table


def spectral_tables(time_count):
    order_n = 7
    points = -np.cos(np.pi * np.arange(order_n + 1) / order_n)
    for _ in range(60):
        legendre = legendre_rows(points, order_n)
        points = points - (points * legendre[:, order_n] - legendre[:, order_n - 1]) / (
            (order_n + 1) * legendre[:, order_n]
        )
    legendre = legendre_rows(points, order_n)
    top_poly = legendre[:, order_n]
    weights = 2.0 / (order_n * (order_n + 1) * top_poly**2)
    derivative = np.zeros((order_n + 1, order_n + 1))
    for i in range(order_n + 1):
        for j in range(order_n + 1):
            if i != j:
                derivative[i, j] = top_poly[i] / (top_poly[j] * (points[i] - points[j]))
    derivative[0, 0] = -order_n * (order_n + 1) / 4.0
    derivative[order_n, order_n] = order_n * (order_n + 1) / 4.0
    stiff_1d = derivative.T @ (weights[:, None] * derivative)
    mass_1d = np.zeros((order_n + 1, order_n + 1))
    mass_1d[np.arange(order_n + 1), np.arange(order_n + 1)] = weights
    stiffness = 0.5 * (
        np.kron(np.kron(stiff_1d, mass_1d), mass_1d)
        + np.kron(np.kron(mass_1d, stiff_1d), mass_1d)
        + np.kron(np.kron(mass_1d, mass_1d), stiff_1d)
    )
    angles = np.pi - np.pi * np.arange(time_count) / (time_count - 1)
    cheb_nodes = np.cos(angles)
    vandermonde = np.cos(np.outer(angles, np.arange(time_count)))
    degree = time_count - 1
    half_ends = np.ones(time_count)
    half_ends[0] = 0.5
    half_ends[degree] = 0.5
    inverse_v = 2.0 / degree * vandermonde.T * half_ends[None, :] * half_ends[:, None]
    integral_table = np.zeros((time_count, time_count))
    integral_table[:, 0] = cheb_nodes + 1.0
    integral_table[:, 1] = 0.5 * (cheb_nodes**2 - 1.0)
    for n in range(2, time_count):
        upper_term = np.cos((n + 1) * angles) / (n + 1) - np.cos((n - 1) * angles) / (n - 1)
        lower_term = (-1.0) ** (n + 1) / (n + 1) - (-1.0) ** (n - 1) / (n - 1)
        integral_table[:, n] = 0.5 * (upper_term - lower_term)
    quadrature = 0.5 * SEGMENT_SPAN * integral_table @ inverse_v
    return stiffness, weights, quadrature


def split(table):
    high = table.astype(ml_dtypes.bfloat16)
    return high, (table - high.astype(np.float64)).astype(ml_dtypes.bfloat16)


def halves(value):
    high = value.astype(jnp.bfloat16)
    return high, (value - high.astype(jnp.float32)).astype(jnp.bfloat16)


def mm(a, b):
    return jnp.dot(a, b, preferred_element_type=jnp.float32)


def mm3(a, b):
    return mm(a[0], b[0]) + (mm(a[1], b[0]) + mm(a[0], b[1]))


def flux_factor(weights):
    def assembled(count, ends):
        table = np.tile(weights, (count, 1))
        shared = weights[0] + weights[-1]
        table[1:, 0] = shared
        table[:-1, -1] = shared
        if not ends:
            table[0, 0] = shared
            table[-1, -1] = shared
        return table

    z, y, x = assembled(EZ_DEV, False), assembled(EY, True), assembled(EX, True)
    mass = 0.125 * np.einsum("ai,bj,ck->abcijk", z, y, x)
    return (-DIFFUSIVITY / mass).reshape(EZ_DEV * EY * EX, NODES).astype(np.float32)


def column(row, mask):
    return jnp.sum(jnp.where(mask, row.astype(jnp.float32), 0.0), axis=1, keepdims=True)


def slots_as_column(slot_row):
    square = (slot_row.shape[1], slot_row.shape[1])
    same = lax.broadcasted_iota(jnp.int32, square, 0) == lax.broadcasted_iota(jnp.int32, square, 1)
    return column(slot_row[...], same).astype(jnp.int32)


def one_hot(mask):
    return mask.astype(jnp.float32).astype(jnp.bfloat16)


def flux_setup(slot_row, mobility):
    square = (slot_row.shape[1], slot_row.shape[1])
    place = slot_row[...] == lax.broadcasted_iota(jnp.int32, square, 0)
    to_store = one_hot(slots_as_column(slot_row) == lax.broadcasted_iota(jnp.int32, square, 1))
    return column(mobility[...], place), one_hot(place), to_store


def flux_block(end_ratio, setup, values, k_high, k_low, factor, rate, up, down):
    natural_mobility, to_natural, to_store = setup
    count, elems = values.shape[0], values.shape[1]
    layer = elems // 2
    position = lax.axis_index("space")
    low_end = jnp.where(position == 0, end_ratio, 1.0).astype(jnp.float32)
    high_end = jnp.where(position == lax.axis_size("space") - 1, end_ratio, 1.0).astype(jnp.float32)
    rows = []
    for t in range(count):
        scaled = halves(values[t])
        rows.append([mm(to_natural, part).astype(jnp.bfloat16) for part in scaled])
    natural = [jnp.concatenate([row[i] for row in rows], axis=0) for i in range(2)]
    flux = mm3(natural, (k_high[...], k_low[...]))

    cube = (elems // 8, 8, 128)
    lane = lax.broadcasted_iota(jnp.int32, cube, 2)
    ex = lax.broadcasted_iota(jnp.int32, cube, 1)
    ey = lax.broadcasted_iota(jnp.int32, cube, 0) % 8
    kx, ky = lane % 8, lane // 8 % 8
    x_next, x_prev = (kx == 7) & (ex < 7), (kx == 0) & (ex > 0)
    y_next, y_prev = (ky == 7) & (ey < 7), (ky == 0) & (ey > 0)
    left = lax.broadcasted_iota(jnp.int32, (layer, 128), 1) < 64
    left_half = lax.broadcasted_iota(jnp.int32, (layer // 2, 128), 1) < 64
    for t in range(count):
        columns = []
        for c in range(4):
            f = flux[t * elems : (t + 1) * elems, c * 128 : (c + 1) * 128]
            f = (f * natural_mobility).reshape(cube)
            f = (
                f
                + jnp.where(x_next, ROLL(ROLL(f, 7, 2), 7, 1), 0.0)
                + jnp.where(x_prev, ROLL(ROLL(f, 121, 2), 1, 1), 0.0)
            )
            after, before = ROLL(f, 56, 2), ROLL(f, 72, 2)
            after = jnp.concatenate([after[1:], after[:1]], axis=0)
            before = jnp.concatenate([before[-1:], before[:-1]], axis=0)
            f = f + jnp.where(y_next, after, 0.0) + jnp.where(y_prev, before, 0.0)
            columns.append(f.reshape(elems, 128) * factor[:, c * 128 : (c + 1) * 128])
        first, last = columns[0], columns[3]
        bottom, top = first[:layer], last[layer:]
        half = layer // 2
        up[t] = jnp.where(left_half, ROLL(top[:half], 64, 1), top[half:])
        down[t] = jnp.where(left_half, bottom[half:], ROLL(bottom[:half], 64, 1))
        first_top = first[layer:] + jnp.where(left, ROLL(last[:layer], 64, 1), 0.0)
        last_bottom = last[:layer] + jnp.where(left, 0.0, ROLL(first[layer:], 64, 1))
        columns[0] = jnp.concatenate([jnp.where(left, bottom * low_end, bottom), first_top], axis=0)
        columns[3] = jnp.concatenate([last_bottom, jnp.where(left, top, top * high_end)], axis=0)
        high, low = halves(jnp.concatenate(columns, axis=1))
        stored = mm(to_store, high) + mm(to_store, low)
        v = values[t]
        rate[t] = REACTION_RATE * (v - v * v * v) + stored


def face_picks(slot_row, layer):
    slots = slots_as_column(slot_row)
    elem = lax.broadcasted_iota(jnp.int32, (2 * layer, layer), 1)
    return [one_hot(slots == elem + first) for first in (0, layer)]


def store_face(picks, face):
    high, low = halves(face)
    columns = []
    for pick in picks:
        columns.append(mm(pick, high) + mm(pick, low))
    left = lax.broadcasted_iota(jnp.int32, columns[0].shape, 1) < 64
    return jnp.where(left, columns[0], 0.0), jnp.where(left, 0.0, columns[1])


def final_kernel(slot_row, base, faces, integral, out, pick_first, pick_last):
    @pl.when(pl.program_id(0) == 0)
    def _():
        pick_first[...], pick_last[...] = face_picks(slot_row, faces.shape[1])

    picks = (pick_first[...], pick_last[...])
    for t in range(integral.shape[0]):
        first, last = store_face(picks, faces[t])
        whole = base[...] + integral[t]
        out[t, :, :128] = whole[:, :128] + first
        out[t, :, 128:384] = whole[:, 128:384]
        out[t, :, 384:] = whole[:, 384:] + last


def exchange_kernel(
    last_row, end_ratio, slot_row, mobility, q_high, q_low, start, *refs
):
    (
    values, k_high, k_low, factor, base, faces, integral_out,
    values_v, k_high_v, k_low_v, factor_v, up, down, integral, held, below, above, increment, arrived, sums, earlier,
    loaded, tables, stored, face_sent, face_got, sent, got, returned, back,
    ) = refs
    n, me = lax.axis_size("tm"), lax.axis_index("tm")
    extent, position = lax.axis_size("space"), lax.axis_index("space")
    count, elems, nodes = held.shape
    rows = arrived.shape[2]
    owners = elems // rows
    mesh_id = pl.DeviceIdType.MESH

    def piece(ref, part, j):
        return ref.at[part, pl.ds(pl.multiple_of(j * rows, 8), rows), :]

    def outward(part, j, source):
        return pltpu.make_async_remote_copy(
            src_ref=piece(increment, part, j),
            dst_ref=arrived.at[part, source],
            send_sem=sent.at[part, j],
            recv_sem=got.at[part, source],
            device_id={"tm": j},
            device_id_type=mesh_id,
        )

    def homeward(part, j, owner):
        return pltpu.make_async_remote_copy(
            src_ref=sums.at[part, j],
            dst_ref=piece(earlier, part, owner),
            send_sem=returned.at[part, j],
            recv_sem=back.at[part, owner],
            device_id={"tm": j},
            device_id_type=mesh_id,
        )

    def face_copy(which, block):
        source, target, step = ((up, below, 1), (down, above, -1))[which]
        these = pl.ds(block * T_BLOCK, T_BLOCK)
        return pltpu.make_async_remote_copy(
            src_ref=source.at[these],
            dst_ref=target.at[these],
            send_sem=face_sent.at[which, block],
            recv_sem=face_got.at[which, block],
            device_id={"space": position + step},
            device_id_type=mesh_id,
        )

    def others(action):
        def one(d, carry):
            action(lax.rem(me + d, n))
            return carry

        lax.fori_loop(1, n, one, 0)

    def when(condition, action):
        pl.when(condition)(action)

    def other_owners(action):
        if owners == n:
            others(action)
        else:
            others(lambda j: when(j < owners, lambda: action(j)))

    def send_increment(part):
        @pl.when(me < n - 1)
        def _():
            other_owners(lambda j: outward(part, j, me).start())

    def scan(part):
        def hand_out(i, running):
            @pl.when(i != me)
            def _():
                sums[part, i] = running
                homeward(part, i, me).start()

            @pl.when(i == me)
            def _():
                piece(earlier, part, me)[...] = running

        def add(i, running):
            @pl.when(i != me)
            def _():
                outward(part, i, i).wait_recv()

            @pl.when(i == me)
            def _():
                arrived[part, i] = piece(increment, part, me)[...]

            running = running + arrived[part, i]
            hand_out(i + 1, running)
            return running

        def own():
            lax.fori_loop(0, n - 1, add, jnp.zeros(arrived.shape[2:], jnp.float32))

        if owners == n:
            own()
        else:
            when(me < owners, own)

    def load(block):
        these = pl.ds(block * T_BLOCK, T_BLOCK)
        return pltpu.make_async_copy(values.at[these], values_v.at[these], loaded.at[block])

    table_copies = [
        pltpu.make_async_copy(source, target, tables.at[k])
        for k, (source, target) in enumerate(
            ((k_high, k_high_v), (k_low, k_low_v), (factor, factor_v))
        )
    ]
    load(0).start()
    for copy in table_copies:
        copy.start()
    for block in range(1, count // T_BLOCK):
        load(block).start()
    barrier = pltpu.get_barrier_semaphore()

    def greet(device):
        pl.semaphore_signal(barrier, inc=1, device_id=device, device_id_type=mesh_id)

    others(lambda j: greet({"tm": j}))
    has_below, has_above = position > 0, position < extent - 1
    when(has_below, lambda: greet({"space": position - 1}))
    when(has_above, lambda: greet({"space": position + 1}))

    setup = flux_setup(slot_row, mobility)
    for copy in table_copies:
        copy.wait()

    def flux(block, carry):
        load(block).wait()
        these = pl.ds(block * T_BLOCK, T_BLOCK)
        flux_block(
            end_ratio, setup, values_v.at[these], k_high_v, k_low_v, factor_v,
            held.at[these], up.at[these], down.at[these],
        )

        @pl.when(block == 0)
        def _():
            nearby = has_below.astype(jnp.int32) + has_above.astype(jnp.int32)
            pl.semaphore_wait(barrier, n - 1 + nearby)

        when(has_above, lambda: face_copy(0, block).start())
        when(has_below, lambda: face_copy(1, block).start())
        return carry

    lax.fori_loop(0, count // T_BLOCK, flux, 0)
    blocks = range(count // T_BLOCK)

    def last_integral(ref, first, last):
        total = last_row[0] * ref[0, :, first:last]
        for t in range(1, count):
            total = total + last_row[t] * ref[t, :, first:last]
        return total

    increment[0] = last_integral(held, 128, 384)
    send_increment(0)

    width = 32

    def store(index):
        these = pl.ds(pl.multiple_of(index * width, 8), width)
        return pltpu.make_async_copy(
            integral.at[:, these, :], integral_out.at[:, these, :], stored.at[index]
        )

    def quadrature(index, carry):
        for k in range(width // 8):
            these = pl.ds(pl.multiple_of(index * width + k * 8, 8), 8)
            part = held[:, these, :].reshape(count * 8, nodes)
            done = mm3((q_high[...], q_low[...]), halves(part))
            integral[:, these, :] = done.reshape(count, 8, nodes)
        store(index).start()
        return carry

    pieces = elems // width
    lax.fori_loop(0, pieces // 2, quadrature, 0)
    outer = (last_integral(held, 0, 128), last_integral(held, 384, 512))

    @pl.when(has_below)
    def _():
        for block in blocks:
            face_copy(0, block).wait_recv()

    @pl.when(position == 0)
    def _():
        below[...] = jnp.zeros_like(below)

    @pl.when(has_above)
    def _():
        for block in blocks:
            face_copy(1, block).wait_recv()

    @pl.when(position == extent - 1)
    def _():
        above[...] = jnp.zeros_like(above)

    def unpacked(lower, upper):
        axis = lower.ndim - 1
        left = lax.broadcasted_iota(jnp.int32, lower.shape, axis) < 64
        near = jnp.where(left, lower, upper)
        far = jnp.where(left, ROLL(lower, 64, axis), ROLL(upper, 64, axis))
        return jnp.concatenate([near, far], axis=axis - 1)

    last_face = unpacked(last_integral(below, 0, 128), last_integral(above, 0, 128))
    first, last = store_face(face_picks(slot_row, last_face.shape[0]), last_face)
    increment[1, :, :128] = outer[0] + first
    increment[1, :, 128:] = outer[1] + last
    send_increment(1)
    scan(0)
    lax.fori_loop(pieces // 2, pieces, quadrature, 0)
    face = unpacked(below[...], above[...])
    for block in range(face.shape[1] // 8):
        part = face[:, block * 8 : block * 8 + 8, :].reshape(count * 8, 128)
        done = mm3((q_high[...], q_low[...]), halves(part))
        faces[:, block * 8 : block * 8 + 8, :] = done.reshape(count, 8, 128)
    scan(1)

    @pl.when(me == 0)
    def _():
        base[...] = start[...]

    @pl.when(me > 0)
    def _():
        for part in range(2):
            other_owners(lambda j: homeward(part, j, j).wait_recv())
        base[:, :128] = start[:, :128] + earlier[1, :, :128]
        base[:, 128:384] = start[:, 128:384] + earlier[0]
        base[:, 384:] = start[:, 384:] + earlier[1, :, 128:]

    for index in range(elems // width):
        store(index).wait()
    for block in blocks:
        when(has_above, lambda: face_copy(0, block).wait_send())
        when(has_below, lambda: face_copy(1, block).wait_send())

    def sent_home(part, j):
        when(j > 0, lambda: homeward(part, j, me).wait_send())

    for part in range(2):

        @pl.when(me < n - 1)
        def _():
            other_owners(lambda j: outward(part, j, me).wait_send())

        def all_home():
            others(lambda j: sent_home(part, j))

        if owners == n:
            all_home()
        else:
            when(me < owners, all_home)


def exchange(end_ratio, slot_row, mobility, quadrature, start_state, values, tables):
    count, elems, nodes = values.shape
    n = lax.axis_size("tm")
    rows = max(8, elems // n)
    q_high, q_low = split(np.kron(quadrature, np.eye(8)))
    f32 = jnp.float32
    piece = pltpu.VMEM((2, n, rows, nodes // 2), f32)
    whole = pltpu.VMEM((2, elems, nodes // 2), f32)
    face = pltpu.VMEM((count, elems // 4, 128), f32)
    field = pltpu.VMEM(values.shape, f32)
    vmem = pl.BlockSpec(memory_space=pltpu.VMEM)
    anywhere = pl.BlockSpec(memory_space=pl.ANY)
    dma = pltpu.SemaphoreType.DMA
    last_row = [float(x) for x in quadrature[-1].astype(np.float32)]
    return pl.pallas_call(
        functools.partial(exchange_kernel, last_row, end_ratio),
        out_shape=(
            jax.ShapeDtypeStruct((elems, nodes), f32),
            jax.ShapeDtypeStruct((count, elems // 2, 128), f32),
            jax.ShapeDtypeStruct(values.shape, f32),
        ),
        in_specs=[vmem] * 5 + [anywhere] * 4,
        out_specs=(vmem, vmem, anywhere),
        scratch_shapes=[
            field,
            pltpu.VMEM((nodes, nodes), jnp.bfloat16),
            pltpu.VMEM((nodes, nodes), jnp.bfloat16),
            pltpu.VMEM((elems, nodes), f32),
            face,
            face,
            field,
            field,
            face,
            face,
            whole,
            piece,
            piece,
            whole,
            dma((count // T_BLOCK,)),
            dma((3,)),
            dma((elems // 32,)),
            dma((2, count // T_BLOCK)),
            dma((2, count // T_BLOCK)),
        ]
        + [dma((2, n))] * 4,
        compiler_params=pltpu.CompilerParams(
            collective_id=0, has_side_effects=True, vmem_limit_bytes=60 * 2**20
        ),
        name="exchange",
    )(slot_row, mobility, q_high, q_low, start_state, values, *tables)


def whole_block(*shape):
    return pl.BlockSpec(shape, lambda i: (0,) * len(shape))


def on_device(iterate, start_state, mobility, slot_element):
    values = iterate[0]
    count, elems, nodes = values.shape
    stiffness, weights, quadrature = spectral_tables(count)
    k_high, k_low = split(stiffness)
    factor = flux_factor(weights)
    end_ratio = float((weights[0] + weights[-1]) / weights[0])
    slot_row = slot_element.reshape(1, elems)
    half = elems // 4
    params = pltpu.CompilerParams(vmem_limit_bytes=60 * 2**20)
    field = jax.ShapeDtypeStruct((count, elems, nodes), jnp.float32)
    times = pl.BlockSpec((FINAL_BLOCK, elems, nodes), lambda i: (i, 0, 0))
    base, faces, integral = exchange(
        end_ratio,
        slot_row,
        mobility.reshape(1, elems),
        quadrature,
        start_state,
        values,
        (k_high, k_low, factor),
    )
    result = pl.pallas_call(
        final_kernel,
        out_shape=field,
        grid=(count // FINAL_BLOCK,),
        in_specs=[
            whole_block(1, elems),
            whole_block(elems, nodes),
            pl.BlockSpec((FINAL_BLOCK, 2 * half, 128), lambda i: (i, 0, 0)),
            times,
        ],
        out_specs=times,
        scratch_shapes=[pltpu.VMEM((elems, 2 * half), jnp.bfloat16)] * 2,
        compiler_params=params,
        name="final",
    )(slot_row, base, faces, integral)
    return result[None]


def solution(mesh):
    in_specs = (P("tm", None, "space", None), P("space", None), P("space"), P("space", None))
    out_specs = P("tm", None, "space", None)
    return jax.shard_map(
        on_device, mesh=mesh, in_specs=in_specs, out_specs=out_specs, check_vma=False
    )
```
